256 devices in a mesh: ctx: 32 (over z, x_lo, core), head: 8 (over y, x_hi).
Axes of the slice: x: 4 (x_hi: 2, x_lo: 2; x = x_hi * 2 + x_lo), y: 4, z: 8, core: 2. Of those that a mesh axis runs over, the one named last changes fastest.
Arguments:
- queries: bfloat16 [4096, 12288], P('ctx', 'head'), may hold values from -65 to 65
- latent: bfloat16 [4096, 576], P('ctx'), may hold values from -5 to 5
- w_uk: bfloat16 [64, 128, 512], P('head'), may hold values from -0.75 to 0.75
- w_uv: bfloat16 [64, 512, 128], P('head'), may hold values from -1.5 to 1.5
- w_out: bfloat16 [8192, 3584], P('head'), may hold values from -0.0625 to 0.0625
- span_ids: int32 [64], P('ctx'), may hold values from 0 to 63, each once
- seq_lengths: int32 [4], replicated, may hold values from 1 to 2048, 4096 in all
Outputs:
- mixed: bfloat16 [4096, 3584], P(('ctx', 'head'))
The draws below stay inside these ranges and needn't reach their ends.
Inputs may be any that keep to these rules, and one draw needn't show every extreme that they name: `span_ids`: each of the 64 block numbers once. `seq_lengths`: they sum to 4096; the longest is 2048.
All inputs are finite; a program needn't handle non-finite values.
Results may differ from the reference program's by a relative error of at most 0.019.
Values may be sent and summed in bfloat16 or wider, within the bound.
A program may use at most 64 MiB of HBM per device.

```python
import math
import jax
import jax.numpy as jnp
import numpy as np
from jax import lax

HEADS = 64
NOPE = 128
ROPE = 64
LAT = 512
VDIM = 128
D_OUT = 3584
SEQS = 4
TOK_DEV = 128
TOKENS = 4096
SPANS = 64


def draw_latent(key, part):
    key = jax.random.fold_in(key, 1)
    first_key, second_key = jax.random.split(key)
    latent_part = jax.random.truncated_normal(first_key, -5.0, 5.0, (TOKENS, LAT), jnp.float32)
    rope_part = jax.random.truncated_normal(second_key, -5.0, 5.0, (TOKENS, ROPE), jnp.float32)
    return jnp.concatenate([latent_part, rope_part], axis=1).astype(jnp.bfloat16)


def draw_queries(key, part):
    key = jax.random.fold_in(key, 2)
    base = jax.random.truncated_normal(key, -5.0, 5.0, (TOKENS, HEADS, NOPE + ROPE), jnp.float32)
    return base.reshape(TOKENS, HEADS * (NOPE + ROPE)).astype(jnp.bfloat16)


def shard_levels(stream_key, shape, shards, smallest, top_value):
    factor_of = 1.0
    for position, shards_of in shards:
        steps = jax.random.uniform(jax.random.fold_in(jax.random.fold_in(stream_key, 6), position), (shards_of,), jnp.float32, smallest / len(shards), top_value / len(shards))
        factor_of = factor_of * jnp.repeat(jnp.exp(steps), shape[position] // shards_of).reshape((-1,) + (1,) * (len(shape) - 1 - position))
    return factor_of


def profile(amount, total, most, lean):
    portions = [(1 << 20) // math.isqrt(grade ** lean) + 1 for grade in range(2, amount + 1)]
    spare, counts = total - most - (amount - 1), [1] * (amount - 1)
    while spare > 0:
        movable = [i for i in range(amount - 1) if counts[i] < most]
        pool, left = sum([portions[i] for i in movable]), spare
        for i in movable:
            more = min(most - counts[i], max(1, left * portions[i] // pool), spare)
            counts[i] = counts[i] + more
            spare = spare - more
    return np.array([most] + counts)


def uneven(stream_key, count, total, reach, skew):
    if count == 2:
        one = jax.random.randint(stream_key, (), max(1, total - reach), min(reach, total - 1) + 1)
        return jnp.stack([one, total - one])
    tallies = jnp.asarray(profile(count, total, reach, skew), jnp.int32)
    pairs = (count - 1) // 2
    source_of, sink = tallies[1:1 + 2 * pairs:2], tallies[2:2 + 2 * pairs:2]
    room = jnp.minimum(source_of - 1, reach - sink)
    passed = jax.random.randint(jax.random.fold_in(stream_key, 1), (pairs,), 0, 1 << 20) % (room + 1)
    tallies = tallies.at[1:1 + 2 * pairs:2].set(source_of - passed).at[2:2 + 2 * pairs:2].set(sink + passed)
    return tallies[jax.random.permutation(jax.random.fold_in(stream_key, 2), count)]


def bell_draw(own_key, shape, scale, reach, cuts=(), kind=jnp.bfloat16):
    result = jax.random.normal(own_key, shape, jnp.float32) * scale
    if len(cuts) > 0:
        result = shard_levels(own_key, shape, cuts, -0.22, 0.18) * result
    return jnp.clip(result, min=-reach, max=reach).astype(kind)


def setup_inputs(seed: int = 0) -> dict:
    key_of = jax.random.split(jax.random.key(seed), 8)
    queries = draw_queries(jax.random.fold_in(key_of[7], 71), 0)
    latent = draw_latent(jax.random.fold_in(key_of[7], 71), 0)
    w_uk = bell_draw(key_of[2], (HEADS, NOPE, LAT), (NOPE // 2) ** -0.5, 0.75, ((0, 8),))
    w_uv = bell_draw(key_of[3], (HEADS, LAT, VDIM), (LAT // 32) ** -0.5, 1.5, ((0, 8),))
    w_out = bell_draw(key_of[4], (HEADS * VDIM, D_OUT), (HEADS * VDIM) ** -0.5, 0.0625, ((0, 8),))
    span_ids = jax.random.permutation(key_of[5], SPANS).astype(jnp.int32)
    seq_lengths = uneven(key_of[6], SEQS, TOKENS, TOKENS // 2, 2).astype(jnp.int32)
    return {"queries": queries, "latent": latent, "w_uk": w_uk, "w_uv": w_uv, "w_out": w_out, "span_ids": span_ids, "seq_lengths": seq_lengths}


def segment_of(positions, seq_lengths):
    seq_ends = jnp.cumsum(seq_lengths).astype(jnp.int32)
    return lax.optimization_barrier(jnp.sum((seq_ends[None, :] <= positions[:, None]).astype(jnp.int32), axis=1))

def reference(queries, latent, w_uk, w_uv, w_out, span_ids, seq_lengths):
    half_rows = TOK_DEV // 2
    all_rows = jnp.arange(TOKENS, dtype=jnp.int32)
    positions = span_ids[all_rows // half_rows].astype(jnp.int32) * half_rows + all_rows % half_rows
    segments = segment_of(positions, seq_lengths)
    shaped = queries.reshape(TOKENS, HEADS, NOPE + ROPE)
    q_abs = jnp.einsum('thn,hnl->thl', shaped[:, :, :NOPE].astype(jnp.float32), w_uk.astype(jnp.float32)).astype(jnp.bfloat16)
    q_rope = shaped[:, :, NOPE:].astype(jnp.float32)
    latent_keys = latent[:, :LAT].astype(jnp.float32)
    rope_keys = latent[:, LAT:].astype(jnp.float32)
    score_scale = 1.0 / math.sqrt(NOPE + ROPE)
    block_rows = TOK_DEV

    def one_block(first_row):
        qa_block = lax.dynamic_slice_in_dim(q_abs, first_row, block_rows, 0).astype(jnp.float32)
        qr_block = lax.dynamic_slice_in_dim(q_rope, first_row, block_rows, 0)
        pos_block = lax.dynamic_slice_in_dim(positions, first_row, block_rows, 0)
        seg_block = lax.dynamic_slice_in_dim(segments, first_row, block_rows, 0)
        scores = (jnp.einsum('thl,kl->thk', qa_block, latent_keys) + jnp.einsum('thr,kr->thk', qr_block, rope_keys)) * score_scale
        visible = (positions[None, :] <= pos_block[:, None]) & (segments[None, :] == seg_block[:, None])
        scores = jnp.where(visible[:, None, :], scores, -1e+30)
        top_score = lax.optimization_barrier(jnp.max(scores, axis=2))
        weights = jnp.where(visible[:, None, :], jnp.exp(scores - top_score[:, :, None]), 0.0)
        mass = lax.optimization_barrier(jnp.sum(weights, axis=2))
        rounded = weights.astype(jnp.bfloat16).astype(jnp.float32)
        accum = jnp.einsum('thk,kl->thl', rounded, latent_keys)
        return (accum / mass[:, :, None]).astype(jnp.bfloat16)
    starts = jnp.arange(0, TOKENS, block_rows, dtype=jnp.int32)
    context = lax.map(one_block, starts).reshape(TOKENS, HEADS, LAT)
    attended = jnp.einsum('thl,hlv->thv', context.astype(jnp.float32), w_uv.astype(jnp.float32)).astype(jnp.bfloat16)
    attended = attended.reshape(TOKENS, HEADS * VDIM)
    return jnp.dot(attended, w_out, preferred_element_type=jnp.float32).astype(jnp.bfloat16)
```

```python
import functools
import math

import jax
import jax.numpy as jnp
from jax import lax
from jax.experimental import pallas as pl
from jax.experimental.pallas import tpu as pltpu
from jax.sharding import PartitionSpec as P

MESH = pl.DeviceIdType.MESH
LOW = -1e30
F32 = jnp.float32
BF16 = jnp.bfloat16

PIECE = 96
HALF = 48
ROWS = 144


def coords():
    c = lax.axis_index("ctx")
    h = lax.axis_index("head")
    return (h % 2) * 2 + (c // 2) % 2, h // 2, c // 4, c % 2


def device(x, y, z, k):
    x = (x + 4) % 4
    y = (y + 4) % 4
    z = (z + 8) % 8
    k = k % 2
    return (z * 4 + (x % 2) * 2 + k, y * 2 + x // 2)


def gather_kernel(
    q_ref, latent_ref, w_uk_ref, ids_ref, g_ref, qk_ref, ids_out_ref, own, tags, send_sem, recv_sem, tag_send, tag_recv, local_sem
):
    x, y, z, k = coords()
    xlo = x % 2
    up = device(x, y, z + 1, k)
    down = device(x, y, z - 1, k)
    xp = device(x + 1, y, z, k)
    xm = device(x - 1, y, z, k)
    yp = device(x, y + 1, z, k)
    ym = device(x, y - 1, z, k)
    sib = device(x, y, z, k + 1)

    def block(dz, other_x=0):
        return k * 16 + ((z + dz + 8) % 8) * 2 + (xlo + other_x) % 2

    def pair(dz):
        if dz == 0:
            return pl.ds(block(0, 1), 1)
        return pl.ds(k * 16 + ((z + dz + 8) % 8) * 2, 2)

    lat = latent_ref[...]
    own[0:64, :] = lat[0:64, :512]
    rope = lat[:, 512:576].astype(F32)
    packed = jnp.concatenate([rope[0:64], rope[64:128]], axis=1).astype(BF16)
    for q in range(4):
        own[64:80, 128 * q : 128 * q + 128] = packed[16 * q : 16 * q + 16, :]
    for u in range(4):
        own[pl.ds(pl.multiple_of(80 + 16 * ((u - y + 4) % 4), 16), 16), :] = lat[64 + 16 * u : 80 + 16 * u, :512]
    row = lax.broadcasted_iota(jnp.int32, (8, 128), 1)
    tags[k, xlo, z] = jnp.where(row == 0, ids_ref[0], ids_ref[1])

    barrier = pltpu.get_barrier_semaphore()
    for d in (up, down, xp, xm, yp, ym, sib):
        pl.semaphore_signal(barrier, inc=1, device_id=d, device_id_type=MESH)
    pl.semaphore_wait(barrier, 7)

    copies = {}

    def send(name, src, dst, dev):
        n = len(copies)
        cp = pltpu.make_async_remote_copy(
            src_ref=src, dst_ref=dst, send_sem=send_sem.at[n], recv_sem=recv_sem.at[n], device_id=dev, device_id_type=MESH
        )
        cp.start()
        copies[name] = cp

    def got(name):
        copies[name].wait_recv()

    tag_copies = []

    def send_tag(ref, dev):
        n = len(tag_copies)
        cp = pltpu.make_async_remote_copy(
            src_ref=ref, dst_ref=ref, send_sem=tag_send.at[n], recv_sem=tag_recv.at[n], device_id=dev, device_id_type=MESH
        )
        cp.start()
        tag_copies.append(cp)
        return cp

    def tag(dz):
        return tags.at[k, xlo, (z + dz + 8) % 8]

    first = pl.ds(0, PIECE)
    lo = pl.ds(0, HALF)
    hi = pl.ds(HALF, HALF)

    def fwd(name, dz, dev, rows=first, other_x=0):
        ref = g_ref.at[block(dz, other_x), rows]
        send(name, ref, ref, dev)

    g0 = block(0)
    send("zu1", own.at[first], g_ref.at[g0, first], up)
    send("zd1", own.at[first], g_ref.at[g0, first], down)
    send("xm0", own.at[lo], g_ref.at[g0, lo], xp)
    send("xp0", own.at[hi], g_ref.at[g0, hi], xm)
    send("s0", own, g_ref.at[g0], sib)
    local = pltpu.make_async_copy(own, g_ref.at[g0], local_sem)
    local.start()
    tu = send_tag(tag(0), up)
    td = send_tag(tag(0), down)

    def queries(h):
        qn = q_ref[:, 192 * h : 192 * h + 128]
        qr = q_ref[:, 192 * h + 128 : 192 * h + 192].astype(F32)
        qa = jnp.dot(qn, w_uk_ref[h], preferred_element_type=F32).astype(BF16)
        qr = jnp.concatenate([qr, qr], axis=1).astype(BF16)
        for s in range(2):
            qk_ref[s, 64 * h : 64 * h + 64, 0:512] = qa[64 * s : 64 * s + 64]
            qk_ref[s, 64 * h : 64 * h + 64, 512:640] = qr[64 * s : 64 * s + 64]

    for h in range(8):
        queries(h)

    def y_out(dz):
        src = g_ref.at[pair(dz), pl.ds(80, 16)]
        send(f"ym{dz}", src, g_ref.at[pair(dz), pl.ds(128, 16)], yp)
        send(f"yp{dz}", src, g_ref.at[pair(dz), pl.ds(96, 16)], ym)

    def y_relay(dz):
        if dz <= 0:
            got(f"ym{dz}")
            send(f"yr{dz}", g_ref.at[pair(dz), pl.ds(128, 16)], g_ref.at[pair(dz), pl.ds(112, 16)], yp)
        else:
            got(f"yp{dz}")
            send(f"yr{dz}", g_ref.at[pair(dz), pl.ds(96, 16)], g_ref.at[pair(dz), pl.ds(112, 16)], ym)

    def y_done(dz):
        got(f"yp{dz}" if dz <= 0 else f"ym{dz}")
        got(f"yr{dz}")
        ref = g_ref.at[pair(dz), pl.ds(96, 48)]
        send(f"sy{dz}", ref, ref, sib)

    def z_step(n):
        if n < 4:
            got(f"zu{n}")
            if n < 3:
                fwd(f"zu{n + 1}", -n, up)
            else:
                fwd("zu4", -n, up, lo)
            fwd(f"xm{n}", -n, xp)
            got(f"zd{n}")
            if n < 3:
                fwd(f"zd{n + 1}", n, down)
            else:
                fwd("zd4", n, down, hi)
            fwd(f"xp{n}", n, xm)
            fwd(f"s{-n}", -n, sib)
            fwd(f"s{n}", n, sib)
        else:
            got("zu4")
            fwd("xm4", 4, xp, lo)
            got("zd4")
            fwd("xp4", 4, xm, hi)
            fwd("s4", 4, sib)

    def x_step(n):
        if n in (0, 4):
            got(f"xm{n}")
            got(f"xp{n}")
            y_out(n)
            fwd(f"sx{n}", n, sib, first, 1)
        else:
            got(f"xm{n}")
            y_out(-n)
            got(f"xp{n}")
            y_out(n)
            fwd(f"sx{-n}", -n, sib, first, 1)
            fwd(f"sx{n}", n, sib, first, 1)

    def tag_step(n):
        nonlocal tu, td
        tu.wait_recv()
        if n < 4:
            tu = send_tag(tag(-n), up)
            td.wait_recv()
            if n < 3:
                td = send_tag(tag(n), down)

    z_step(1)
    tag_step(1)
    local.wait()
    x_step(0)
    z_step(2)
    tag_step(2)
    x_step(1)
    y_relay(0)
    z_step(3)
    tag_step(3)
    x_step(2)
    y_relay(-1)
    y_relay(1)
    y_done(0)
    z_step(4)
    tag_step(4)
    tx = send_tag(tags.at[k, xlo], xp)
    x_step(3)
    y_relay(-2)
    y_relay(2)
    y_done(-1)
    y_done(1)
    x_step(4)
    tx.wait_recv()
    ts = send_tag(tags.at[k], sib)
    y_relay(-3)
    y_relay(3)
    y_done(-2)
    y_done(2)
    y_relay(4)
    y_done(-3)
    y_done(3)
    y_done(4)
    ts.wait_recv()
    for c in range(32):
        ids_out_ref[c : c + 1, :] = tags[c // 16, (c // 8) % 2, c % 8, 0:1, :]
    for dz in (0, -1, 1, -2, 2, -3, 3, 4):
        got(f"s{dz}")
        got(f"sx{dz}")
    for dz in (0, -1, 1, -2, 2, -3, 3, 4):
        got(f"sy{dz}")
    for cp in copies.values():
        cp.wait_send()
    for cp in tag_copies:
        cp.wait_send()


def gather(queries, latent, w_uk, span_ids):
    vmem = pl.BlockSpec(memory_space=pltpu.VMEM)
    return pl.pallas_call(
        gather_kernel,
        name="gather",
        out_shape=(
            jax.ShapeDtypeStruct((32, ROWS, 512), BF16),
            jax.ShapeDtypeStruct((2, 512, 640), BF16),
            jax.ShapeDtypeStruct((32, 128), jnp.int32),
        ),
        in_specs=[vmem, vmem, vmem, pl.BlockSpec(memory_space=pltpu.SMEM)],
        out_specs=(vmem, vmem, vmem),
        scratch_shapes=[
            pltpu.VMEM((ROWS, 512), BF16),
            pltpu.VMEM((2, 2, 8, 8, 128), jnp.int32),
            pltpu.SemaphoreType.DMA((72,)),
            pltpu.SemaphoreType.DMA((72,)),
            pltpu.SemaphoreType.DMA((9,)),
            pltpu.SemaphoreType.DMA((9,)),
            pltpu.SemaphoreType.DMA,
        ],
        compiler_params=pltpu.CompilerParams(collective_id=1, has_side_effects=True, vmem_limit_bytes=24 << 20),
    )(queries, latent, w_uk, span_ids)


GROUP = 4
KEYS = 64 * GROUP


def attend_kernel(scale, ids_ref, my_ref, len_ref, g_ref, qk_ref, w_uv_ref, out_ref, where_ref, kbuf, acc, ctx):
    y = lax.axis_index("head") // 2
    for c in range(32):
        for s in range(2):
            where_ref[ids_ref[c, s]] = 2 * ((c // 16) * 16 + (c % 8) * 2 + (c // 8) % 2) + s
    ends = []
    total = 0
    for j in range(4):
        total = total + len_ref[j]
        ends.append(total)
    log2e = scale * math.log2(math.e)
    lane = lax.broadcasted_iota(jnp.int32, (64, 128), 1)
    col = lax.broadcasted_iota(jnp.int32, (1, KEYS), 1)
    tok = lax.broadcasted_iota(jnp.int32, (64, 1), 0)

    for s in range(2):
        i = my_ref[s]
        pos_q = i * 64 + tok
        start_q = jnp.zeros((64, 1), jnp.int32)
        first = jnp.int32(0)
        for e in ends[:3]:
            start_q = jnp.where(pos_q >= e, e, start_q)
            first = jnp.where(i * 64 >= e, e, first)
        j_low = first // 64
        groups = (i - j_low) // GROUP + 1

        def step(m, carry):
            top, mass = carry
            base = i - GROUP * m
            pos_k = jnp.zeros((1, KEYS), jnp.int32)
            for u in range(GROUP):
                j = base - u
                place = where_ref[jnp.maximum(j, 0)]
                b = place // 2
                half = place % 2
                turn = y * half
                row = pl.multiple_of(80 * half, 16)
                kbuf[64 * u : 64 * u + 64, 0:512] = g_ref[b, pl.ds(row, 64), :]
                for p in range(4):
                    tile = g_ref[b, 64:80, pl.ds(pl.multiple_of(128 * ((p + turn) % 4), 128), 128)]
                    kbuf[64 * u + 16 * p : 64 * u + 16 * p + 16, 512:640] = jnp.where(
                        lane[0:16] // 64 == half, tile, jnp.zeros_like(tile)
                    )
                off = col - 64 * u
                off = (off + 16 * turn) % 64
                pos_k = jnp.where(col // 64 == u, j * 64 + off, pos_k)
            bias = jnp.where((pos_k <= pos_q) & (pos_k >= start_q), 0.0, LOW).astype(F32)
            keys = kbuf[...]
            sc = lax.dot_general(qk_ref[s], keys, (((1,), (1,)), ((), ())), preferred_element_type=F32)
            sc = (sc.reshape(8, 64, KEYS) + bias[None]).reshape(512, KEYS)
            top_new = jnp.maximum(top, jnp.max(sc, axis=1, keepdims=True))
            w = jnp.exp2((sc - top_new) * log2e)
            fade = jnp.exp2((top - top_new) * log2e)
            mass = mass * fade + w[:, 0:128] + w[:, 128:256]
            acc[...] = acc[...] * fade + jnp.dot(w.astype(BF16), keys[:, 0:512], preferred_element_type=F32)
            return top_new, mass

        acc[...] = jnp.zeros_like(acc)
        top, mass = lax.fori_loop(
            0, groups, step, (jnp.full((512, 1), LOW, F32), jnp.zeros((512, 128), F32))
        )
        total_mass = jnp.sum(mass, axis=1, keepdims=True)
        done = (acc[...] / total_mass).astype(BF16)
        for h in range(8):
            ctx[h, 64 * s : 64 * s + 64, :] = done[64 * h : 64 * h + 64]

    for h in range(8):
        out_ref[:, 128 * h : 128 * h + 128] = jnp.dot(ctx[h], w_uv_ref[h], preferred_element_type=F32).astype(BF16)


def attend(ids, span_ids, seq_lengths, g, qk, w_uv, scale):
    vmem = pl.BlockSpec(memory_space=pltpu.VMEM)
    smem = pl.BlockSpec(memory_space=pltpu.SMEM)
    return pl.pallas_call(
        functools.partial(attend_kernel, scale),
        name="attend",
        out_shape=jax.ShapeDtypeStruct((128, 1024), BF16),
        in_specs=[smem, smem, smem, vmem, vmem, vmem],
        out_specs=vmem,
        scratch_shapes=[
            pltpu.SMEM((64,), jnp.int32),
            pltpu.VMEM((KEYS, 640), BF16),
            pltpu.VMEM((512, 512), F32),
            pltpu.VMEM((8, 128, 512), BF16),
        ],
        compiler_params=pltpu.CompilerParams(vmem_limit_bytes=24 << 20),
    )(ids, span_ids, seq_lengths, g, qk, w_uv)


CHUNK = 512


def project_kernel(att_ref, w_ref, out_ref, part, got, send_sem, recv_sem):
    x, y, z, k = coords()
    xh = x // 2
    others = [(dx, dy) for dy in (2, 1, 3, 0) for dx in (1, 0) if (dx, dy) != (0, 0)]
    peers = [device(x + 2 * dx, y + dy, z, k) for dx, dy in others]
    me = y * 2 + xh

    barrier = pltpu.get_barrier_semaphore()
    for d in peers:
        pl.semaphore_signal(barrier, inc=1, device_id=d, device_id_type=MESH)
    pl.semaphore_wait(barrier, len(peers))

    copies = []
    chunks = 3584 // CHUNK
    for c in range(chunks):
        cols = slice(CHUNK * c, CHUNK * c + CHUNK)
        part[:, cols] = jnp.dot(att_ref[...], w_ref[:, cols], preferred_element_type=F32).astype(BF16)
        for n, d in enumerate(peers):
            copy = pltpu.make_async_remote_copy(
                src_ref=part.at[pl.ds(pl.multiple_of(16 * d[1], 16), 16), pl.ds(CHUNK * c, CHUNK)],
                dst_ref=got.at[n, :, pl.ds(CHUNK * c, CHUNK)],
                send_sem=send_sem.at[c, n],
                recv_sem=recv_sem.at[c, n],
                device_id=d,
                device_id_type=MESH,
            )
            copy.start()
            copies.append(copy)
    for c in range(chunks):
        cols = slice(CHUNK * c, CHUNK * c + CHUNK)
        total = part[pl.ds(pl.multiple_of(16 * me, 16), 16), cols].astype(F32)
        for n in range(len(peers)):
            copies[c * len(peers) + n].wait_recv()
            total = total + got[n, :, cols].astype(F32)
        out_ref[:, cols] = total.astype(BF16)
    for copy in copies:
        copy.wait_send()


def project(attended, w_out):
    vmem = pl.BlockSpec(memory_space=pltpu.VMEM)
    return pl.pallas_call(
        project_kernel,
        name="project",
        out_shape=jax.ShapeDtypeStruct((16, 3584), BF16),
        in_specs=[vmem, vmem],
        out_specs=vmem,
        scratch_shapes=[
            pltpu.VMEM((128, 3584), BF16),
            pltpu.VMEM((7, 16, 3584), BF16),
            pltpu.SemaphoreType.DMA((3584 // CHUNK, 7)),
            pltpu.SemaphoreType.DMA((3584 // CHUNK, 7)),
        ],
        compiler_params=pltpu.CompilerParams(collective_id=2, has_side_effects=True, vmem_limit_bytes=24 << 20),
    )(attended, w_out)


def shards(queries, latent, w_uk, w_uv, w_out, span_ids, seq_lengths):
    scale = 1.0 / math.sqrt(queries.shape[1] // w_uk.shape[0])
    g, qk, ids = gather(queries, latent, w_uk, span_ids)
    attended = attend(ids, span_ids, seq_lengths, g, qk, w_uv, scale)
    return project(attended, w_out)


def solution(mesh):
    return jax.shard_map(
        shards,
        mesh=mesh,
        in_specs=(
            P("ctx", "head"),
            P("ctx", None),
            P("head", None, None),
            P("head", None, None),
            P("head", None),
            P("ctx"),
            P(),
        ),
        out_specs=P(("ctx", "head"), None),
        check_vma=False,
    )
```

```python
import functools
import math

import jax
import jax.numpy as jnp
from jax import lax
from jax.experimental import pallas as pl
from jax.experimental.pallas import tpu as pltpu
from jax.sharding import PartitionSpec as P

MESH = pl.DeviceIdType.MESH
LOW = -1e30
F32 = jnp.float32
BF16 = jnp.bfloat16

ROWS = 144


def coords():
    c = lax.axis_index("ctx")
    h = lax.axis_index("head")
    return (h % 2) * 2 + (c // 2) % 2, h // 2, c // 4, c % 2


def device(x, y, z, k):
    x = (x + 4) % 4
    y = (y + 4) % 4
    z = (z + 8) % 8
    k = k % 2
    return (z * 4 + (x % 2) * 2 + k, y * 2 + x // 2)


def in_hbm(array):
    return pltpu.with_memory_space_constraint(array, pltpu.HBM)


def gather_kernel(
    q_hbm, latent_hbm, w_uk_hbm, ids_hbm, g_ref, qk_ref, ids_out_ref,
    own, tags, q_ref, lat_ref, w_uk_ref, ids_ref, send_sem, recv_sem, tag_send, tag_recv, local_sem,
):
    x, y, z, k = coords()
    xlo = x % 2
    zs = {n: device(x, y, z + n, k) for n in (1, -1, 2, -2, 3, -3, 4)}
    up, down = zs[1], zs[-1]
    xp = device(x + 1, y, z, k)
    xm = device(x - 1, y, z, k)
    ys = {n: device(x, y + n, z, k) for n in (1, 2, 3)}
    sib = device(x, y, z, k + 1)

    barrier = pltpu.get_barrier_semaphore()
    friends = (*zs.values(), xp, xm, *ys.values(), sib)
    for d in friends:
        pl.semaphore_signal(barrier, inc=1, device_id=d, device_id_type=MESH)

    loads = []
    for n, (src, dst) in enumerate(((latent_hbm, lat_ref), (ids_hbm, ids_ref), (q_hbm, q_ref), (w_uk_hbm, w_uk_ref))):
        cp = pltpu.make_async_copy(src, dst, local_sem.at[n])
        cp.start()
        loads.append(cp)

    loads[0].wait()
    lat = lat_ref[...].T
    for q in range(4):
        own[q, 0:128, :] = lat[:, 128 * q : 128 * q + 128]
    rope = lat[:, 512:576].astype(F32)
    packed = jnp.concatenate([rope[0:64], rope[64:128]], axis=1).astype(BF16)
    for q in range(4):
        own[q, 128:144, :] = packed[16 * q : 16 * q + 16, :]
    loads[1].wait()
    col = lax.broadcasted_iota(jnp.int32, (8, 128), 1)
    tags[k, xlo, z] = jnp.where(col == 0, ids_ref[0], ids_ref[1])

    pl.semaphore_wait(barrier, len(friends))

    copies = {}

    def send(name, src, dst, dev):
        n = len(copies)
        cp = pltpu.make_async_remote_copy(
            src_ref=src, dst_ref=dst, send_sem=send_sem.at[n], recv_sem=recv_sem.at[n], device_id=dev, device_id_type=MESH
        )
        cp.start()
        copies[name] = cp

    def got(name):
        copies[name].wait_recv()

    tag_copies = []

    def send_tag(ref, dev):
        n = len(tag_copies)
        cp = pltpu.make_async_remote_copy(
            src_ref=ref, dst_ref=ref, send_sem=tag_send.at[n], recv_sem=tag_recv.at[n], device_id=dev, device_id_type=MESH
        )
        cp.start()
        tag_copies.append(cp)

    def block(dz, other_x=0):
        return k * 16 + ((z + dz + 8) % 8) * 2 + (xlo + other_x) % 2

    def whole(dz, other_x=0):
        return g_ref.at[:, block(dz, other_x)]

    def fwd(name, ref, dev):
        send(name, ref, ref, dev)

    def quarter(dz, other_x=0):
        return g_ref.at[y, block(dz, other_x)]

    def y_out(dz, other_x):
        for n in (2, 1, 3):
            fwd(f"y{n}:{dz},{other_x}", quarter(dz, other_x), ys[n])

    def y_done(dz, other_x):
        for n in (1, 3, 2):
            got(f"y{n}:{dz},{other_x}")
        fwd(f"s:{dz},{other_x}", whole(dz, other_x), sib)

    g0 = block(0)
    for n in (3, -3, 4):
        send(f"z:{-n if n < 4 else 4}", own.at[y], g_ref.at[y, g0], zs[n])
    send("z:-1", own, whole(0), up)
    send("z:1", own, whole(0), down)
    send("x0a", own.at[0:2], g_ref.at[0:2, g0], xp)
    send("x0b", own.at[2:4], g_ref.at[2:4, g0], xm)
    send("s:0,0", own, whole(0), sib)
    local = pltpu.make_async_copy(own, whole(0), local_sem.at[4])
    local.start()
    for n in (3, -3, 4, 2, -2, 1, -1):
        send_tag(tags.at[k, xlo, z], zs[n])

    loads[2].wait()
    loads[3].wait()

    def queries(h):
        qn = q_ref[:, 192 * h : 192 * h + 128]
        qr = q_ref[:, 192 * h + 128 : 192 * h + 192].astype(F32)
        qa = jnp.dot(qn, w_uk_ref[h], preferred_element_type=F32).astype(BF16)
        qr = jnp.concatenate([qr, qr], axis=1).astype(BF16)
        for s in range(2):
            qk_ref[s, 64 * h : 64 * h + 64, 0:512] = qa[64 * s : 64 * s + 64]
            qk_ref[s, 64 * h : 64 * h + 64, 512:640] = qr[64 * s : 64 * s + 64]

    for h in range(8):
        queries(h)

    got("z:-3")
    y_out(-3, 0)
    fwd("x:-3", quarter(-3), xp)
    got("z:3")
    y_out(3, 0)
    fwd("x:3", quarter(3), xm)
    got("z:4")
    y_out(4, 0)
    fwd("x4a", quarter(4).at[0:80], xp)
    fwd("x4b", quarter(4).at[80:144], xm)
    got("z:-1")
    fwd("z:-2", whole(-1), up)
    fwd("x:-1", whole(-1), xp)
    fwd("s:-1,0", whole(-1), sib)
    got("z:1")
    fwd("z:2", whole(1), down)
    fwd("x:1", whole(1), xm)
    fwd("s:1,0", whole(1), sib)
    got("x0a")
    got("x0b")
    fwd("s:0,1", whole(0, 1), sib)
    for n in range(7):
        tag_copies[n].wait_recv()
    send_tag(tags.at[k, xlo], xp)
    got("x:-3")
    y_out(-3, 1)
    got("x:3")
    y_out(3, 1)
    got("x4a")
    got("x4b")
    y_out(4, 1)
    got("z:-2")
    fwd("x:-2", whole(-2), xp)
    fwd("s:-2,0", whole(-2), sib)
    got("z:2")
    fwd("x:2", whole(2), xm)
    fwd("s:2,0", whole(2), sib)
    got("x:-1")
    fwd("s:-1,1", whole(-1, 1), sib)
    got("x:1")
    fwd("s:1,1", whole(1, 1), sib)
    tag_copies[7].wait_recv()
    send_tag(tags.at[k], sib)
    y_done(-3, 0)
    y_done(3, 0)
    y_done(4, 0)
    got("x:-2")
    fwd("s:-2,1", whole(-2, 1), sib)
    got("x:2")
    fwd("s:2,1", whole(2, 1), sib)
    y_done(-3, 1)
    y_done(3, 1)
    y_done(4, 1)
    tag_copies[8].wait_recv()
    for c in range(32):
        ids_out_ref[c : c + 1, :] = tags[c // 16, (c // 8) % 2, c % 8, 0:1, :]
    for dz in (0, -1, 1, -2, 2, -3, 3, 4):
        for other_x in range(2):
            got(f"s:{dz},{other_x}")
    local.wait()
    for cp in copies.values():
        cp.wait_send()
    for cp in tag_copies:
        cp.wait_send()


def gather(queries, latent, w_uk, span_ids):
    vmem = pl.BlockSpec(memory_space=pltpu.VMEM)
    hbm = pl.BlockSpec(memory_space=pl.ANY)
    return pl.pallas_call(
        gather_kernel,
        name="gather",
        out_shape=(
            jax.ShapeDtypeStruct((4, 32, ROWS, 128), BF16),
            jax.ShapeDtypeStruct((2, 512, 640), BF16),
            jax.ShapeDtypeStruct((32, 128), jnp.int32),
        ),
        in_specs=[hbm, hbm, hbm, hbm],
        out_specs=(vmem, vmem, vmem),
        scratch_shapes=[
            pltpu.VMEM((4, ROWS, 128), BF16),
            pltpu.VMEM((2, 2, 8, 8, 128), jnp.int32),
            pltpu.VMEM((128, 1536), BF16),
            pltpu.VMEM((576, 128), BF16),
            pltpu.VMEM((8, 128, 512), BF16),
            pltpu.SMEM((2,), jnp.int32),
            pltpu.SemaphoreType.DMA((51,)),
            pltpu.SemaphoreType.DMA((51,)),
            pltpu.SemaphoreType.DMA((9,)),
            pltpu.SemaphoreType.DMA((9,)),
            pltpu.SemaphoreType.DMA((5,)),
        ],
        compiler_params=pltpu.CompilerParams(collective_id=1, has_side_effects=True, vmem_limit_bytes=24 << 20),
    )(*map(in_hbm, (queries, latent.T, w_uk, span_ids)))


GROUP = 8
KEYS = 64 * GROUP


def attend_kernel(
    scale, ids_ref, my_hbm, len_hbm, g_ref, qk_ref, w_uv_hbm, out_ref, where_ref, my_ref, len_ref, kbuf, acc, ctx, w_uv_ref, sem
):
    loads = []
    for n, (src, dst) in enumerate(((my_hbm, my_ref), (len_hbm, len_ref), (w_uv_hbm, w_uv_ref))):
        cp = pltpu.make_async_copy(src, dst, sem.at[n])
        cp.start()
        loads.append(cp)
    for c in range(32):
        for s in range(2):
            where_ref[ids_ref[c, s]] = 2 * ((c // 16) * 16 + (c % 8) * 2 + (c // 8) % 2) + s
    loads[0].wait()
    loads[1].wait()
    ends = []
    total = 0
    for j in range(4):
        total = total + len_ref[j]
        ends.append(total)
    log2e = scale * math.log2(math.e)
    lane = lax.broadcasted_iota(jnp.int32, (16, 128), 1)
    col = lax.broadcasted_iota(jnp.int32, (1, KEYS), 1)
    tok = lax.broadcasted_iota(jnp.int32, (64, 1), 0)

    for s in range(2):
        i = my_ref[s]
        pos_q = i * 64 + tok
        start_q = jnp.zeros((64, 1), jnp.int32)
        first = jnp.int32(0)
        for e in ends[:3]:
            start_q = jnp.where(pos_q >= e, e, start_q)
            first = jnp.where(i * 64 >= e, e, first)
        j_low = first // 64
        groups = (i - j_low) // GROUP + 1

        def step(m, carry):
            top, mass = carry
            base = i - GROUP * m
            pos_k = jnp.zeros((1, KEYS), jnp.int32)
            for u in range(GROUP):
                j = base - u
                place = where_ref[jnp.maximum(j, 0)]
                b = place // 2
                half = place % 2
                row = pl.multiple_of(64 * half, 64)
                for q in range(4):
                    kbuf[64 * u : 64 * u + 64, 128 * q : 128 * q + 128] = g_ref[q, b, pl.ds(row, 64), :]
                    tile = g_ref[q, b, 128:144, :]
                    kbuf[64 * u + 16 * q : 64 * u + 16 * q + 16, 512:640] = jnp.where(
                        lane // 64 == half, tile, jnp.zeros_like(tile)
                    )
                pos_k = jnp.where(col // 64 == u, j * 64 + col % 64, pos_k)
            bias = jnp.where((pos_k <= pos_q) & (pos_k >= start_q), 0.0, LOW).astype(F32)
            keys = kbuf[...]
            sc = lax.dot_general(qk_ref[s], keys, (((1,), (1,)), ((), ())), preferred_element_type=F32)
            sc = (sc.reshape(8, 64, KEYS) + bias[None]).reshape(512, KEYS)
            top_new = jnp.maximum(top, jnp.max(sc, axis=1, keepdims=True))
            w = jnp.exp2((sc - top_new) * log2e)
            fade = jnp.exp2((top - top_new) * log2e)
            mass = mass * fade + sum(w[:, 128 * e : 128 * e + 128] for e in range(KEYS // 128))
            acc[...] = acc[...] * fade + jnp.dot(w.astype(BF16), keys[:, 0:512], preferred_element_type=F32)
            return top_new, mass

        acc[...] = jnp.zeros_like(acc)
        top, mass = lax.fori_loop(
            0, groups, step, (jnp.full((512, 1), LOW, F32), jnp.zeros((512, 128), F32))
        )
        total_mass = jnp.sum(mass, axis=1, keepdims=True)
        done = (acc[...] / total_mass).astype(BF16)
        for h in range(8):
            ctx[h, 64 * s : 64 * s + 64, :] = done[64 * h : 64 * h + 64]

    loads[2].wait()
    for h in range(8):
        out_ref[:, 128 * h : 128 * h + 128] = jnp.dot(ctx[h], w_uv_ref[h], preferred_element_type=F32).astype(BF16)


def attend(ids, span_ids, seq_lengths, g, qk, w_uv, scale):
    vmem = pl.BlockSpec(memory_space=pltpu.VMEM)
    smem = pl.BlockSpec(memory_space=pltpu.SMEM)
    hbm = pl.BlockSpec(memory_space=pl.ANY)
    return pl.pallas_call(
        functools.partial(attend_kernel, scale),
        name="attend",
        out_shape=jax.ShapeDtypeStruct((128, 1024), BF16),
        in_specs=[smem, hbm, hbm, vmem, vmem, hbm],
        out_specs=vmem,
        scratch_shapes=[
            pltpu.SMEM((64,), jnp.int32),
            pltpu.SMEM((2,), jnp.int32),
            pltpu.SMEM((4,), jnp.int32),
            pltpu.VMEM((KEYS, 640), BF16),
            pltpu.VMEM((512, 512), F32),
            pltpu.VMEM((8, 128, 512), BF16),
            pltpu.VMEM((8, 512, 128), BF16),
            pltpu.SemaphoreType.DMA((3,)),
        ],
        compiler_params=pltpu.CompilerParams(vmem_limit_bytes=24 << 20),
    )(ids, in_hbm(span_ids), in_hbm(seq_lengths), g, qk, in_hbm(w_uv))


CHUNK = 512


def project_kernel(att_ref, w_ref, out_ref, part, got, send_sem, recv_sem):
    x, y, z, k = coords()
    xh = x // 2
    others = [(dx, dy) for dy in (2, 1, 3, 0) for dx in (1, 0) if (dx, dy) != (0, 0)]
    peers = [device(x + 2 * dx, y + dy, z, k) for dx, dy in others]
    me = y * 2 + xh

    barrier = pltpu.get_barrier_semaphore()
    for d in peers:
        pl.semaphore_signal(barrier, inc=1, device_id=d, device_id_type=MESH)
    pl.semaphore_wait(barrier, len(peers))

    copies = []
    chunks = 3584 // CHUNK
    for c in range(chunks):
        cols = slice(CHUNK * c, CHUNK * c + CHUNK)
        part[:, cols] = jnp.dot(att_ref[...], w_ref[:, cols], preferred_element_type=F32).astype(BF16)
        for n, d in enumerate(peers):
            copy = pltpu.make_async_remote_copy(
                src_ref=part.at[pl.ds(pl.multiple_of(16 * d[1], 16), 16), pl.ds(CHUNK * c, CHUNK)],
                dst_ref=got.at[n, :, pl.ds(CHUNK * c, CHUNK)],
                send_sem=send_sem.at[c, n],
                recv_sem=recv_sem.at[c, n],
                device_id=d,
                device_id_type=MESH,
            )
            copy.start()
            copies.append(copy)
    for c in range(chunks):
        cols = slice(CHUNK * c, CHUNK * c + CHUNK)
        total = part[pl.ds(pl.multiple_of(16 * me, 16), 16), cols].astype(F32)
        for n in range(len(peers)):
            copies[c * len(peers) + n].wait_recv()
            total = total + got[n, :, cols].astype(F32)
        out_ref[:, cols] = total.astype(BF16)
    for copy in copies:
        copy.wait_send()


def project(attended, w_out):
    vmem = pl.BlockSpec(memory_space=pltpu.VMEM)
    return pl.pallas_call(
        project_kernel,
        name="project",
        out_shape=jax.ShapeDtypeStruct((16, 3584), BF16),
        in_specs=[vmem, vmem],
        out_specs=vmem,
        scratch_shapes=[
            pltpu.VMEM((128, 3584), BF16),
            pltpu.VMEM((7, 16, 3584), BF16),
            pltpu.SemaphoreType.DMA((3584 // CHUNK, 7)),
            pltpu.SemaphoreType.DMA((3584 // CHUNK, 7)),
        ],
        compiler_params=pltpu.CompilerParams(collective_id=2, has_side_effects=True, vmem_limit_bytes=24 << 20),
    )(attended, w_out)


def shards(queries, latent, w_uk, w_uv, w_out, span_ids, seq_lengths):
    scale = 1.0 / math.sqrt(queries.shape[1] // w_uk.shape[0])
    g, qk, ids = gather(queries, latent, w_uk, span_ids)
    attended = attend(ids, span_ids, seq_lengths, g, qk, w_uv, scale)
    return project(attended, w_out)


def solution(mesh):
    return jax.shard_map(
        shards,
        mesh=mesh,
        in_specs=(
            P("ctx", "head"),
            P("ctx", None),
            P("head", None, None),
            P("head", None, None),
            P("head", None),
            P("ctx"),
            P(),
        ),
        out_specs=P(("ctx", "head"), None),
        check_vma=False,
    )
```

```python
import functools
import math

import jax
import jax.numpy as jnp
from jax import lax
from jax.experimental import pallas as pl
from jax.experimental.pallas import tpu as pltpu
from jax.sharding import PartitionSpec as P

MESH = pl.DeviceIdType.MESH
LOW = -1e30
CHUNK = 512
F32 = jnp.float32
BF16 = jnp.bfloat16

ROWS = 144


def coords():
    c = lax.axis_index("ctx")
    h = lax.axis_index("head")
    return (h % 2) * 2 + (c // 2) % 2, h // 2, c // 4, c % 2


def device(x, y, z, k):
    x = (x + 4) % 4
    y = (y + 4) % 4
    z = (z + 8) % 8
    k = k % 2
    return (z * 4 + (x % 2) * 2 + k, y * 2 + x // 2)


def in_hbm(array):
    return pltpu.with_memory_space_constraint(array, pltpu.HBM)


def fused_kernel(
    log2e, q_hbm, latent_hbm, w_uk_hbm, w_uv_hbm, w_out_hbm, ids_hbm, len_hbm, out_ref,
    g_ref, own, tags, mate, q_ref, lat_ref, w_uk_ref, w_uv_ref, w_out_ref, ids_ref, len_ref,
    qt, keys_ref, acc, top, mass, att, part, shares,
    send_sem, recv_sem, tag_send, tag_recv, share_send, share_recv, local_sem,
):
    x, y, z, k = coords()
    xlo = x % 2
    zs = {n: device(x, y, z + n, k) for n in (1, -1, 2, -2, 3, -3, 4)}
    up, down = zs[1], zs[-1]
    xp = device(x + 1, y, z, k)
    xm = device(x - 1, y, z, k)
    ys = {n: device(x, y + n, z, k) for n in (1, 2, 3)}
    sib = device(x, y, z, k + 1)
    peers = [ys[2], ys[1], ys[3]] + [device(x + 2, y + n, z, k) for n in (2, 1, 3, 0)]

    barrier = pltpu.get_barrier_semaphore()
    friends = (*zs.values(), xp, xm, sib, *peers)
    for d in friends:
        pl.semaphore_signal(barrier, inc=1, device_id=d, device_id_type=MESH)

    loads = []
    for n, (src, dst) in enumerate(
        (
            (latent_hbm, lat_ref),
            (ids_hbm, ids_ref),
            (len_hbm, len_ref),
            (q_hbm, q_ref),
            (w_uk_hbm, w_uk_ref),
            (w_uv_hbm, w_uv_ref),
            (w_out_hbm, w_out_ref),
        )
    ):
        cp = pltpu.make_async_copy(src, dst, local_sem.at[n])
        cp.start()
        loads.append(cp)

    loads[0].wait()
    lat = lat_ref[...].T
    for q in range(4):
        own[q, 0:128, :] = lat[:, 128 * q : 128 * q + 128]
    rope = lat[:, 512:576].astype(F32)
    packed = jnp.concatenate([rope[0:64], rope[64:128]], axis=1).astype(BF16)
    for q in range(4):
        own[q, 128:144, :] = packed[16 * q : 16 * q + 16, :]
    loads[1].wait()
    col = lax.broadcasted_iota(jnp.int32, (8, 128), 1)
    tags[k, xlo, z] = jnp.where(col < 64, ids_ref[0] * 64 + col, ids_ref[1] * 64 + col - 64)

    pl.semaphore_wait(barrier, len(friends))

    copies = {}

    def send(name, src, dst, dev):
        n = len(copies)
        cp = pltpu.make_async_remote_copy(
            src_ref=src, dst_ref=dst, send_sem=send_sem.at[n], recv_sem=recv_sem.at[n], device_id=dev, device_id_type=MESH
        )
        cp.start()
        copies[name] = cp

    def got(name):
        copies[name].wait_recv()

    tag_copies = []

    def send_tag(ref, dev, to=None):
        n = len(tag_copies)
        cp = pltpu.make_async_remote_copy(
            src_ref=ref, dst_ref=ref if to is None else to, send_sem=tag_send.at[n], recv_sem=tag_recv.at[n], device_id=dev, device_id_type=MESH
        )
        cp.start()
        tag_copies.append(cp)

    def place(dz, other_x=0, other_core=0):
        return (k + other_core) % 2, (xlo + other_x) % 2, (z + dz + 8) % 8

    def block(dz, other_x=0, other_core=0):
        core, xl, zz = place(dz, other_x, other_core)
        return core * 16 + zz * 2 + xl

    def whole(dz, other_x=0):
        return g_ref.at[:, block(dz, other_x)]

    def fwd(name, ref, dev):
        send(name, ref, ref, dev)

    def quarter(dz, other_x=0):
        return g_ref.at[y, block(dz, other_x)]

    def y_out(dz, other_x):
        for n in (2, 1, 3):
            fwd(f"y{n}:{dz},{other_x}", quarter(dz, other_x), ys[n])

    def y_done(dz, other_x):
        for n in (1, 3, 2):
            got(f"y{n}:{dz},{other_x}")
        fwd(f"s:{dz},{other_x}", whole(dz, other_x), sib)

    g0 = block(0)
    for n in (3, -3, 4):
        send(f"z:{-n if n < 4 else 4}", own.at[y], g_ref.at[y, g0], zs[n])
    send("x0a", own.at[0:2], g_ref.at[0:2, g0], xp)
    send("x0b", own.at[2:4], g_ref.at[2:4, g0], xm)
    send("s:0,0", own, whole(0), sib)
    for n in (3, -3, 4, 2, -2, 1, -1):
        send_tag(tags.at[k, xlo, z], zs[n])
    send_tag(tags.at[k, xlo, z], sib, mate)
    send("z:-1", own, whole(0), up)
    send("z:1", own, whole(0), down)

    loads[3].wait()
    loads[4].wait()
    for h in range(8):
        qn = q_ref[:, 192 * h : 192 * h + 128]
        qr = q_ref[:, 192 * h + 128 : 192 * h + 192].astype(F32)
        qa = jnp.dot(qn, w_uk_ref[h], preferred_element_type=F32).astype(BF16)
        qr = jnp.concatenate([qr, qr], axis=1).astype(BF16)
        qt[0:512, 128 * h : 128 * h + 128] = qa.T
        qt[512:640, 128 * h : 128 * h + 128] = qr.T

    loads[2].wait()
    pos_q = tags[k, xlo, z, 0:1, :]
    start_q = jnp.zeros((1, 128), jnp.int32)
    end = jnp.int32(0)
    for j in range(3):
        end = end + len_ref[j]
        start_q = jnp.where(pos_q >= end, end, start_q)

    acc[...] = jnp.zeros_like(acc)
    top[...] = jnp.full_like(top, LOW)
    mass[...] = jnp.zeros_like(mass)
    lane = lax.broadcasted_iota(jnp.int32, (16, 128), 1)
    row = lax.broadcasted_iota(jnp.int32, (128, 1), 0)

    def absorb(places, mine=False):
        amount = 128 * len(places)
        biases = []
        for n, p in enumerate(places):
            b = block(*p)
            for q in range(4):
                if mine and n == 0:
                    feats, tile = own[q, 0:128, :], own[q, 128:144, :]
                else:
                    feats, tile = g_ref[q, b, 0:128, :], g_ref[q, b, 128:144, :]
                keys_ref[128 * n : 128 * n + 128, 128 * q : 128 * q + 128] = feats
                zero = jnp.zeros_like(tile)
                r = 128 * n + 16 * q
                keys_ref[r : r + 16, 512:640] = jnp.where(lane < 64, tile, zero)
                keys_ref[r + 64 : r + 80, 512:640] = jnp.where(lane < 64, zero, tile)
            tag = mate if mine and n == 1 else tags.at[place(*p)]
            pos_k = jnp.where(row < 64, tag[0:1, 0:1] + row, tag[0:1, 64:65] + row - 64)
            biases.append(jnp.where((pos_k <= pos_q) & (pos_k >= start_q), 0.0, LOW).astype(F32))
        bias = jnp.concatenate(biases, axis=0)
        keys = keys_ref[0:amount, :]
        scores = jnp.dot(keys, qt[...], preferred_element_type=F32) + jnp.concatenate([bias] * 8, axis=1)
        top_old = top[...]
        top_new = jnp.maximum(top_old, jnp.max(scores, axis=0, keepdims=True))
        weights = jnp.exp2((scores - top_new) * log2e)
        fade = jnp.exp2((top_old - top_new) * log2e)
        mass[...] = mass[...] * fade + jnp.sum(weights, axis=0, keepdims=True)
        acc[...] = acc[...] * fade + lax.dot_general(
            keys[:, 0:512], weights.astype(BF16), (((0,), (0,)), ((), ())), preferred_element_type=F32
        )
        top[...] = top_new

    def absorb_both(*places):
        absorb([(dz, ox, c) for dz, ox in places for c in range(2)])

    def sib_got(*places):
        for dz, ox in places:
            got(f"s:{dz},{ox}")

    sib_got((0, 0))
    tag_copies[7].wait_recv()
    absorb([(0, 0, 0), (0, 0, 1)], mine=True)
    got("z:-3")
    y_out(-3, 0)
    fwd("x:-3", quarter(-3), xp)
    got("z:3")
    y_out(3, 0)
    fwd("x:3", quarter(3), xm)
    got("z:4")
    y_out(4, 0)
    fwd("x4a", quarter(4).at[0:80], xp)
    fwd("x4b", quarter(4).at[80:144], xm)
    got("x0a")
    got("x0b")
    fwd("s:0,1", whole(0, 1), sib)
    for n in range(7):
        tag_copies[n].wait_recv()
    send_tag(tags.at[k, xlo], xp)
    got("z:-1")
    fwd("z:-2", whole(-1), up)
    fwd("x:-1", whole(-1), xp)
    fwd("s:-1,0", whole(-1), sib)
    got("z:1")
    fwd("z:2", whole(1), down)
    fwd("x:1", whole(1), xm)
    fwd("s:1,0", whole(1), sib)
    tag_copies[8].wait_recv()
    send_tag(tags.at[k], sib)
    got("x:-3")
    y_out(-3, 1)
    got("x:3")
    y_out(3, 1)
    got("x4a")
    got("x4b")
    y_out(4, 1)
    tag_copies[9].wait_recv()
    sib_got((0, 1))
    absorb_both((0, 1))
    got("z:-2")
    fwd("x:-2", whole(-2), xp)
    fwd("s:-2,0", whole(-2), sib)
    got("z:2")
    fwd("x:2", whole(2), xm)
    fwd("s:2,0", whole(2), sib)
    got("x:-1")
    fwd("s:-1,1", whole(-1, 1), sib)
    got("x:1")
    fwd("s:1,1", whole(1, 1), sib)
    sib_got((-1, 0), (1, 0))
    absorb_both((-1, 0), (1, 0))
    y_done(-3, 0)
    y_done(3, 0)
    y_done(4, 0)
    sib_got((-2, 0), (2, 0))
    absorb_both((-2, 0), (2, 0))
    sib_got((-1, 1), (1, 1))
    absorb_both((-1, 1), (1, 1))
    y_done(-3, 1)
    y_done(3, 1)
    y_done(4, 1)
    got("x:-2")
    fwd("s:-2,1", whole(-2, 1), sib)
    got("x:2")
    fwd("s:2,1", whole(2, 1), sib)
    sib_got((-3, 0), (3, 0))
    absorb_both((-3, 0), (3, 0))
    sib_got((4, 0), (4, 1))
    absorb_both((4, 0), (4, 1))
    sib_got((-3, 1), (3, 1))
    absorb_both((-3, 1), (3, 1))
    sib_got((-2, 1), (2, 1))
    absorb_both((-2, 1), (2, 1))

    loads[5].wait()
    for h in range(8):
        cols = slice(128 * h, 128 * h + 128)
        context = (acc[:, cols] / mass[:, cols]).astype(BF16)
        att[:, cols] = lax.dot_general(
            context, w_uv_ref[h], (((0,), (0,)), ((), ())), preferred_element_type=F32
        ).astype(BF16)

    loads[6].wait()
    me = device(x, y, z, k)[1]
    chunks = 3584 // CHUNK
    sent = []
    for c in range(chunks):
        cols = slice(CHUNK * c, CHUNK * c + CHUNK)
        part[:, cols] = jnp.dot(att[...], w_out_ref[:, cols], preferred_element_type=F32).astype(BF16)
        for n, d in enumerate(peers):
            cp = pltpu.make_async_remote_copy(
                src_ref=part.at[pl.ds(pl.multiple_of(16 * d[1], 16), 16), pl.ds(CHUNK * c, CHUNK)],
                dst_ref=shares.at[n, :, pl.ds(CHUNK * c, CHUNK)],
                send_sem=share_send.at[c, n],
                recv_sem=share_recv.at[c, n],
                device_id=d,
                device_id_type=MESH,
            )
            cp.start()
            sent.append(cp)
    for cp in copies.values():
        cp.wait_send()
    for cp in tag_copies:
        cp.wait_send()
    for c in range(chunks):
        cols = slice(CHUNK * c, CHUNK * c + CHUNK)
        total = part[pl.ds(pl.multiple_of(16 * me, 16), 16), cols].astype(F32)
        for n in range(len(peers)):
            sent[c * len(peers) + n].wait_recv()
            total = total + shares[n, :, cols].astype(F32)
        out_ref[:, cols] = total.astype(BF16)
    for cp in sent:
        cp.wait_send()


def shards(queries, latent, w_uk, w_uv, w_out, span_ids, seq_lengths):
    scale = 1.0 / math.sqrt(queries.shape[1] // w_uk.shape[0])
    hbm = pl.BlockSpec(memory_space=pl.ANY)
    chunks = 3584 // CHUNK
    dma = pltpu.SemaphoreType.DMA
    return pl.pallas_call(
        functools.partial(fused_kernel, scale * math.log2(math.e)),
        name="fused",
        out_shape=jax.ShapeDtypeStruct((16, 3584), BF16),
        in_specs=[hbm] * 7,
        out_specs=pl.BlockSpec(memory_space=pltpu.VMEM),
        scratch_shapes=[
            pltpu.VMEM((4, 32, ROWS, 128), BF16),
            pltpu.VMEM((4, ROWS, 128), BF16),
            pltpu.VMEM((2, 2, 8, 8, 128), jnp.int32),
            pltpu.VMEM((8, 128), jnp.int32),
            pltpu.VMEM((128, 1536), BF16),
            pltpu.VMEM((576, 128), BF16),
            pltpu.VMEM((8, 128, 512), BF16),
            pltpu.VMEM((8, 512, 128), BF16),
            pltpu.VMEM((1024, 3584), BF16),
            pltpu.SMEM((2,), jnp.int32),
            pltpu.SMEM((4,), jnp.int32),
            pltpu.VMEM((640, 1024), BF16),
            pltpu.VMEM((512, 640), BF16),
            pltpu.VMEM((512, 1024), F32),
            pltpu.VMEM((1, 1024), F32),
            pltpu.VMEM((1, 1024), F32),
            pltpu.VMEM((128, 1024), BF16),
            pltpu.VMEM((128, 3584), BF16),
            pltpu.VMEM((7, 16, 3584), BF16),
            dma((51,)),
            dma((51,)),
            dma((10,)),
            dma((10,)),
            dma((chunks, 7)),
            dma((chunks, 7)),
            dma((7,)),
        ],
        compiler_params=pltpu.CompilerParams(collective_id=1, has_side_effects=True, vmem_limit_bytes=48 << 20),
    )(*map(in_hbm, (queries, latent.T, w_uk, w_uv, w_out, span_ids, seq_lengths)))


def solution(mesh):
    return jax.shard_map(
        shards,
        mesh=mesh,
        in_specs=(
            P("ctx", "head"),
            P("ctx", None),
            P("head", None, None),
            P("head", None, None),
            P("head", None),
            P("ctx"),
            P(),
        ),
        out_specs=P(("ctx", "head"), None),
        check_vma=False,
    )
```

```python
import functools
import math

import jax
import jax.numpy as jnp
from jax import lax
from jax.experimental import pallas as pl
from jax.experimental.pallas import tpu as pltpu
from jax.sharding import PartitionSpec as P

MESH = pl.DeviceIdType.MESH
LOW = -1e30
CHUNK = 512
F32 = jnp.float32
BF16 = jnp.bfloat16

ROWS = 144


def coords():
    c = lax.axis_index("ctx")
    h = lax.axis_index("head")
    return (h % 2) * 2 + (c // 2) % 2, h // 2, c // 4, c % 2


def device(x, y, z, k):
    x = (x + 4) % 4
    y = (y + 4) % 4
    z = (z + 8) % 8
    k = k % 2
    return (z * 4 + (x % 2) * 2 + k, y * 2 + x // 2)


def in_hbm(array):
    return pltpu.with_memory_space_constraint(array, pltpu.HBM)


def fused_kernel(
    log2e, q_hbm, latent_hbm, w_uk_hbm, w_uv_hbm, w_out_hbm, ids_hbm, len_hbm, out_ref,
    g_ref, own, tags, mate, q_ref, lat_ref, w_uk_ref, w_uv_ref, w_out_ref, ids_ref, len_ref,
    qt, keys_ref, acc, top, mass, att, part, shares,
    send_sem, recv_sem, tag_send, tag_recv, share_send, share_recv, local_sem,
):
    x, y, z, k = coords()
    xlo = x % 2
    zs = {n: device(x, y, z + n, k) for n in (1, -1, 2, -2, 3, -3, 4)}
    up, down = zs[1], zs[-1]
    xp = device(x + 1, y, z, k)
    xm = device(x - 1, y, z, k)
    ys = {n: device(x, y + n, z, k) for n in (1, 2, 3)}
    sib = device(x, y, z, k + 1)
    peers = [ys[2], ys[1], ys[3]] + [device(x + 2, y + n, z, k) for n in (2, 1, 3, 0)]

    barrier = pltpu.get_barrier_semaphore()
    friends = (*zs.values(), xp, xm, sib, *peers)
    for d in friends:
        pl.semaphore_signal(barrier, inc=1, device_id=d, device_id_type=MESH)

    loads = []
    for n, (src, dst) in enumerate(
        (
            (latent_hbm, lat_ref),
            (ids_hbm, ids_ref),
            (len_hbm, len_ref),
            (q_hbm, q_ref),
            (w_uk_hbm, w_uk_ref),
            (w_uv_hbm, w_uv_ref),
            (w_out_hbm, w_out_ref),
        )
    ):
        cp = pltpu.make_async_copy(src, dst, local_sem.at[n])
        cp.start()
        loads.append(cp)

    loads[0].wait()
    lat = lat_ref[...].T
    for q in range(4):
        own[q, 0:128, :] = lat[:, 128 * q : 128 * q + 128]
    rope = lat[:, 512:576].astype(F32)
    packed = jnp.concatenate([rope[0:64], rope[64:128]], axis=1).astype(BF16)
    for q in range(4):
        own[q, 128:144, :] = packed[16 * q : 16 * q + 16, :]
    loads[1].wait()
    col = lax.broadcasted_iota(jnp.int32, (8, 128), 1)
    tags[k, xlo, z] = jnp.where(col < 64, ids_ref[0] * 64 + col, ids_ref[1] * 64 + col - 64)

    pl.semaphore_wait(barrier, len(friends))

    copies = {}

    def send(name, src, dst, dev):
        n = len(copies)
        cp = pltpu.make_async_remote_copy(
            src_ref=src, dst_ref=dst, send_sem=send_sem.at[n], recv_sem=recv_sem.at[n], device_id=dev, device_id_type=MESH
        )
        cp.start()
        copies[name] = cp

    def got(name):
        copies[name].wait_recv()

    tag_copies = []

    def send_tag(ref, dev, to=None):
        n = len(tag_copies)
        cp = pltpu.make_async_remote_copy(
            src_ref=ref, dst_ref=ref if to is None else to, send_sem=tag_send.at[n], recv_sem=tag_recv.at[n], device_id=dev, device_id_type=MESH
        )
        cp.start()
        tag_copies.append(cp)

    def place(dz, other_x=0, other_core=0):
        return (k + other_core) % 2, (xlo + other_x) % 2, (z + dz + 8) % 8

    def block(dz, other_x=0, other_core=0):
        core, xl, zz = place(dz, other_x, other_core)
        return core * 16 + zz * 2 + xl

    def whole(dz, other_x=0):
        return g_ref.at[:, block(dz, other_x)]

    def fwd(name, ref, dev):
        send(name, ref, ref, dev)

    def quarter(dz, other_x=0):
        return g_ref.at[y, block(dz, other_x)]

    def y_out(dz, other_x):
        for n in (2, 1, 3):
            fwd(f"y{n}:{dz},{other_x}", quarter(dz, other_x), ys[n])

    def y_done(dz, other_x):
        for n in (1, 3, 2):
            got(f"y{n}:{dz},{other_x}")
        fwd(f"s:{dz},{other_x}", whole(dz, other_x), sib)

    g0 = block(0)
    for n in (3, -3, 4, 2, -2, 1, -1):
        send_tag(tags.at[k, xlo, z], zs[n])
    send_tag(tags.at[k, xlo, z], sib, mate)
    send("z:-1", own, whole(0), up)
    send("z:1", own, whole(0), down)
    send("x0a", own.at[0:2], g_ref.at[0:2, g0], xp)
    send("x0b", own.at[2:4], g_ref.at[2:4, g0], xm)
    send("s:0,0", own, whole(0), sib)
    for n in (3, -3, 4):
        send(f"z:{-n if n < 4 else 4}", own.at[y], g_ref.at[y, g0], zs[n])

    loads[3].wait()
    loads[4].wait()
    for h in range(8):
        qn = q_ref[:, 192 * h : 192 * h + 128]
        qr = q_ref[:, 192 * h + 128 : 192 * h + 192].astype(F32)
        qa = jnp.dot(qn, w_uk_ref[h], preferred_element_type=F32).astype(BF16)
        qr = jnp.concatenate([qr, qr], axis=1).astype(BF16)
        qt[0:512, 128 * h : 128 * h + 128] = qa.T
        qt[512:640, 128 * h : 128 * h + 128] = qr.T

    loads[2].wait()
    pos_q = tags[k, xlo, z, 0:1, :]
    start_q = jnp.zeros((1, 128), jnp.int32)
    end = jnp.int32(0)
    for j in range(3):
        end = end + len_ref[j]
        start_q = jnp.where(pos_q >= end, end, start_q)

    token = lax.broadcasted_iota(jnp.int32, (128, 128), 1)
    own_token = (lax.broadcasted_iota(jnp.int32, (128, 128), 0) == token).astype(F32).astype(BF16)
    for h in range(8):
        qt[640:768, 128 * h : 128 * h + 128] = own_token
    acc[...] = jnp.zeros_like(acc)
    top[...] = jnp.full_like(top, LOW)
    mass[...] = jnp.zeros_like(mass)
    lane = lax.broadcasted_iota(jnp.int32, (16, 128), 1)
    row = lax.broadcasted_iota(jnp.int32, (128, 1), 0)

    def absorb(places, mine=False):
        amount = 128 * len(places)
        for n, p in enumerate(places):
            b = block(*p)
            for q in range(4):
                if mine and n == 0:
                    feats, tile = own[q, 0:128, :], own[q, 128:144, :]
                else:
                    feats, tile = g_ref[q, b, 0:128, :], g_ref[q, b, 128:144, :]
                keys_ref[128 * n : 128 * n + 128, 128 * q : 128 * q + 128] = feats
                zero = jnp.zeros_like(tile)
                r = 128 * n + 16 * q
                keys_ref[r : r + 16, 512:640] = jnp.where(lane < 64, tile, zero)
                keys_ref[r + 64 : r + 80, 512:640] = jnp.where(lane < 64, zero, tile)
            tag = mate if mine and n == 1 else tags.at[place(*p)]
            pos_k = jnp.where(row < 64, tag[0:1, 0:1] + row, tag[0:1, 64:65] + row - 64)
            hidden = jnp.where((pos_k <= pos_q) & (pos_k >= start_q), 0.0, LOW).astype(BF16)
            keys_ref[128 * n : 128 * n + 128, 640:768] = hidden
        keys = keys_ref[0:amount, :]
        scores = jnp.dot(keys, qt[...], preferred_element_type=F32)
        top_old = top[...]
        top_new = jnp.maximum(top_old, jnp.max(scores, axis=0, keepdims=True))
        weights = jnp.exp2((scores - top_new) * log2e)
        fade = jnp.exp2((top_old - top_new) * log2e)
        mass[...] = mass[...] * fade + jnp.sum(weights, axis=0, keepdims=True)
        acc[...] = acc[...] * fade + lax.dot_general(
            keys[:, 0:512], weights.astype(BF16), (((0,), (0,)), ((), ())), preferred_element_type=F32
        )
        top[...] = top_new

    def absorb_both(*places):
        absorb([(dz, ox, c) for dz, ox in places for c in range(2)])

    def sib_got(*places):
        for dz, ox in places:
            got(f"s:{dz},{ox}")

    def z_far():
        for dz, dev in ((-3, xp), (3, xm)):
            got(f"z:{dz}")
            y_out(dz, 0)
            fwd(f"x:{dz}", quarter(dz), dev)
        got("z:4")
        y_out(4, 0)
        fwd("x4a", quarter(4).at[0:80], xp)
        fwd("x4b", quarter(4).at[80:144], xm)

    def x_far():
        for dz in (-3, 3):
            got(f"x:{dz}")
            y_out(dz, 1)
        got("x4a")
        got("x4b")
        y_out(4, 1)

    def z_near(n):
        for dz, ahead, side in ((-n, up, xp), (n, down, xm)):
            got(f"z:{dz}")
            if n == 1:
                fwd(f"z:{2 * dz}", whole(dz), ahead)
            fwd(f"x:{dz}", whole(dz), side)
            fwd(f"s:{dz},0", whole(dz), sib)

    def x_near(n):
        if n == 0:
            got("x0a")
            got("x0b")
            fwd("s:0,1", whole(0, 1), sib)
        else:
            for dz in (-n, n):
                got(f"x:{dz}")
                fwd(f"s:{dz},1", whole(dz, 1), sib)

    def y_far(other_x):
        for dz in (-3, 3, 4):
            y_done(dz, other_x)

    def tags_z():
        for n in range(7):
            tag_copies[n].wait_recv()
        send_tag(tags.at[k, xlo], xp)

    def tags_x():
        tag_copies[8].wait_recv()
        send_tag(tags.at[k], sib)

    def take(*places):
        sib_got(*places)
        absorb_both(*places)

    sib_got((0, 0))
    tag_copies[7].wait_recv()
    absorb([(0, 0, 0), (0, 0, 1)], mine=True)
    x_near(0)
    tags_z()
    z_near(1)
    tags_x()
    tag_copies[9].wait_recv()
    take((0, 1))
    z_far()
    x_near(1)
    take((-1, 0), (1, 0))
    z_near(2)
    x_far()
    take((-1, 1), (1, 1))
    y_far(0)
    take((-2, 0), (2, 0))
    x_near(2)
    take((-3, 0), (3, 0), (4, 0))
    y_far(1)
    take((-2, 1), (2, 1))
    take((-3, 1), (3, 1), (4, 1))

    loads[5].wait()
    for h in range(8):
        cols = slice(128 * h, 128 * h + 128)
        context = (acc[:, cols] * (1.0 / mass[:, cols])).astype(BF16)
        att[:, cols] = lax.dot_general(
            context, w_uv_ref[h], (((0,), (0,)), ((), ())), preferred_element_type=F32
        ).astype(BF16)

    loads[6].wait()
    me = device(x, y, z, k)[1]
    chunks = 3584 // CHUNK
    sent = []
    for c in range(chunks):
        cols = slice(CHUNK * c, CHUNK * c + CHUNK)
        part[:, cols] = jnp.dot(att[...], w_out_ref[:, cols], preferred_element_type=F32).astype(BF16)
        for n, d in enumerate(peers):
            cp = pltpu.make_async_remote_copy(
                src_ref=part.at[pl.ds(pl.multiple_of(16 * d[1], 16), 16), pl.ds(CHUNK * c, CHUNK)],
                dst_ref=shares.at[n, :, pl.ds(CHUNK * c, CHUNK)],
                send_sem=share_send.at[c, n],
                recv_sem=share_recv.at[c, n],
                device_id=d,
                device_id_type=MESH,
            )
            cp.start()
            sent.append(cp)
    for cp in copies.values():
        cp.wait_send()
    for cp in tag_copies:
        cp.wait_send()
    for c in range(chunks):
        cols = slice(CHUNK * c, CHUNK * c + CHUNK)
        total = part[pl.ds(pl.multiple_of(16 * me, 16), 16), cols].astype(F32)
        for n in range(len(peers)):
            sent[c * len(peers) + n].wait_recv()
            total = total + shares[n, :, cols].astype(F32)
        out_ref[:, cols] = total.astype(BF16)
        for n in range(len(peers)):
            sent[c * len(peers) + n].wait_send()


def shards(queries, latent, w_uk, w_uv, w_out, span_ids, seq_lengths):
    scale = 1.0 / math.sqrt(queries.shape[1] // w_uk.shape[0])
    hbm = pl.BlockSpec(memory_space=pl.ANY)
    chunks = 3584 // CHUNK
    dma = pltpu.SemaphoreType.DMA
    return pl.pallas_call(
        functools.partial(fused_kernel, scale * math.log2(math.e)),
        name="fused",
        out_shape=jax.ShapeDtypeStruct((16, 3584), BF16),
        in_specs=[hbm] * 7,
        out_specs=pl.BlockSpec(memory_space=pltpu.VMEM),
        scratch_shapes=[
            pltpu.VMEM((4, 32, ROWS, 128), BF16),
            pltpu.VMEM((4, ROWS, 128), BF16),
            pltpu.VMEM((2, 2, 8, 8, 128), jnp.int32),
            pltpu.VMEM((8, 128), jnp.int32),
            pltpu.VMEM((128, 1536), BF16),
            pltpu.VMEM((576, 128), BF16),
            pltpu.VMEM((8, 128, 512), BF16),
            pltpu.VMEM((8, 512, 128), BF16),
            pltpu.VMEM((1024, 3584), BF16),
            pltpu.SMEM((2,), jnp.int32),
            pltpu.SMEM((4,), jnp.int32),
            pltpu.VMEM((768, 1024), BF16),
            pltpu.VMEM((768, 768), BF16),
            pltpu.VMEM((512, 1024), F32),
            pltpu.VMEM((1, 1024), F32),
            pltpu.VMEM((1, 1024), F32),
            pltpu.VMEM((128, 1024), BF16),
            pltpu.VMEM((128, 3584), BF16),
            pltpu.VMEM((7, 16, 3584), BF16),
            dma((51,)),
            dma((51,)),
            dma((10,)),
            dma((10,)),
            dma((chunks, 7)),
            dma((chunks, 7)),
            dma((7,)),
        ],
        compiler_params=pltpu.CompilerParams(collective_id=1, has_side_effects=True, vmem_limit_bytes=48 << 20),
    )(*map(in_hbm, (queries, latent.T, w_uk, w_uv, w_out, span_ids, seq_lengths)))


def solution(mesh):
    return jax.shard_map(
        shards,
        mesh=mesh,
        in_specs=(
            P("ctx", "head"),
            P("ctx", None),
            P("head", None, None),
            P("head", None, None),
            P("head", None),
            P("ctx"),
            P(),
        ),
        out_specs=P(("ctx", "head"), None),
        check_vma=False,
    )
```

```python
import functools
import math

import jax
import jax.numpy as jnp
from jax import lax
from jax.experimental import pallas as pl
from jax.experimental.pallas import tpu as pltpu
from jax.sharding import PartitionSpec as P

MESH = pl.DeviceIdType.MESH
LOW = -1e30
COLUMNS = ((0, 512), (512, 1536), (1536, 2560), (2560, 3584))
F32 = jnp.float32
BF16 = jnp.bfloat16

ROWS = 144


def coords():
    c = lax.axis_index("ctx")
    h = lax.axis_index("head")
    return (h % 2) * 2 + (c // 2) % 2, h // 2, c // 4, c % 2


def device(x, y, z, k):
    x = (x + 4) % 4
    y = (y + 4) % 4
    z = (z + 8) % 8
    k = k % 2
    return (z * 4 + (x % 2) * 2 + k, y * 2 + x // 2)


def in_hbm(array):
    return pltpu.with_memory_space_constraint(array, pltpu.HBM)


def fused_kernel(
    log2e, q_hbm, latent_hbm, w_uk_hbm, w_uv_hbm, w_out_hbm, ids_hbm, len_hbm, out_ref,
    g_ref, own, tags, mate, q_ref, lat_ref, w_uk_ref, w_uv_ref, w_out_ref, ids_ref, len_ref,
    qt, keys_ref, acc, top, mass, att, part, shares, totals,
    send_sem, recv_sem, tag_send, tag_recv, share_send, share_recv, local_sem,
):
    x, y, z, k = coords()
    xlo = x % 2
    zs = {n: device(x, y, z + n, k) for n in (1, -1, 2, -2, 3, -3, 4)}
    up, down = zs[1], zs[-1]
    xp = device(x + 1, y, z, k)
    xm = device(x - 1, y, z, k)
    ys = {n: device(x, y + n, z, k) for n in (1, 2, 3)}
    sib = device(x, y, z, k + 1)
    peers = [ys[2], ys[1], ys[3]] + [device(x + 2, y + n, z, k) for n in (2, 1, 3, 0)]

    barrier = pltpu.get_barrier_semaphore()
    friends = (*zs.values(), xp, xm, sib, *peers)
    for d in friends:
        pl.semaphore_signal(barrier, inc=1, device_id=d, device_id_type=MESH)

    loads = []
    for n, (src, dst) in enumerate(
        (
            (latent_hbm, lat_ref),
            (ids_hbm, ids_ref),
            (len_hbm, len_ref),
            (q_hbm, q_ref),
            (w_uk_hbm, w_uk_ref),
            (w_uv_hbm, w_uv_ref),
            (w_out_hbm, w_out_ref),
        )
    ):
        cp = pltpu.make_async_copy(src, dst, local_sem.at[n])
        cp.start()
        loads.append(cp)

    loads[0].wait()
    lat = lat_ref[...].T
    for q in range(4):
        own[q, 0:128, :] = lat[:, 128 * q : 128 * q + 128]
    rope = lat[:, 512:576].astype(F32)
    packed = jnp.concatenate([rope[0:64], rope[64:128]], axis=1).astype(BF16)
    for q in range(4):
        own[q, 128:144, :] = packed[16 * q : 16 * q + 16, :]
    loads[1].wait()
    col = lax.broadcasted_iota(jnp.int32, (8, 128), 1)
    tags[k, xlo, z] = jnp.where(col < 64, ids_ref[0] * 64 + col, ids_ref[1] * 64 + col - 64)

    pl.semaphore_wait(barrier, len(friends))

    copies = {}

    def send(name, src, dst, dev):
        n = len(copies)
        cp = pltpu.make_async_remote_copy(
            src_ref=src, dst_ref=dst, send_sem=send_sem.at[n], recv_sem=recv_sem.at[n], device_id=dev, device_id_type=MESH
        )
        cp.start()
        copies[name] = cp

    def got(name):
        copies[name].wait_recv()

    tag_copies = []

    def send_tag(ref, dev, to=None):
        n = len(tag_copies)
        cp = pltpu.make_async_remote_copy(
            src_ref=ref, dst_ref=ref if to is None else to, send_sem=tag_send.at[n], recv_sem=tag_recv.at[n], device_id=dev, device_id_type=MESH
        )
        cp.start()
        tag_copies.append(cp)

    def place(dz, other_x=0, other_core=0):
        return (k + other_core) % 2, (xlo + other_x) % 2, (z + dz + 8) % 8

    def block(dz, other_x=0, other_core=0):
        core, xl, zz = place(dz, other_x, other_core)
        return core * 16 + zz * 2 + xl

    def whole(dz, other_x=0):
        return g_ref.at[:, block(dz, other_x)]

    def fwd(name, ref, dev):
        send(name, ref, ref, dev)

    def quarter(dz, other_x=0):
        return g_ref.at[y, block(dz, other_x)]

    def y_out(dz, other_x):
        for n in (2, 1, 3):
            fwd(f"y{n}:{dz},{other_x}", quarter(dz, other_x), ys[n])

    def y_done(dz, other_x):
        for n in (1, 3, 2):
            got(f"y{n}:{dz},{other_x}")
        fwd(f"s:{dz},{other_x}", whole(dz, other_x), sib)

    g0 = block(0)
    for n in (3, -3, 4, 2, -2, 1, -1):
        send_tag(tags.at[k, xlo, z], zs[n])
    send_tag(tags.at[k, xlo, z], sib, mate)
    send("z:-1", own, whole(0), up)
    send("z:1", own, whole(0), down)
    send("x0a", own.at[0:2], g_ref.at[0:2, g0], xp)
    send("x0b", own.at[2:4], g_ref.at[2:4, g0], xm)
    send("s:0,0", own, whole(0), sib)
    for n in (3, -3, 4):
        send(f"z:{-n if n < 4 else 4}", own.at[y], g_ref.at[y, g0], zs[n])

    loads[3].wait()
    loads[4].wait()

    def half_of(rows, s):
        return [rows[16 * o + 8 * s : 16 * o + 8 * s + 8] for o in range(8)]

    spot = lax.broadcasted_iota(jnp.int32, (128, 128), 1) % 64
    feature = lax.broadcasted_iota(jnp.int32, (128, 128), 0)
    for pair in range(4):
        feats, ropes = [], []
        for h in (2 * pair, 2 * pair + 1):
            qn = q_ref[:, 192 * h : 192 * h + 128]
            qr = q_ref[:, 192 * h + 128 : 192 * h + 192].astype(F32)
            feats.append(jnp.dot(qn, w_uk_ref[h], preferred_element_type=F32))
            ropes.append(jnp.concatenate([qr, qr], axis=1))
        for s in range(2):
            cols = slice(512 * s + 128 * pair, 512 * s + 128 * pair + 128)
            qa = jnp.concatenate(half_of(feats[0], s) + half_of(feats[1], s), axis=0)
            qr = jnp.concatenate(half_of(ropes[0], s) + half_of(ropes[1], s), axis=0)
            qt[0:512, cols] = qa.astype(BF16).T
            qt[512:640, cols] = qr.astype(BF16).T
            token = 16 * (spot // 8) + 8 * s + spot % 8
            qt[640:768, cols] = (feature == token).astype(F32).astype(BF16)

    loads[2].wait()
    pos_q = tags[k, xlo, z, 0:1, :]
    start_q = jnp.zeros((1, 128), jnp.int32)
    end = jnp.int32(0)
    for j in range(3):
        end = end + len_ref[j]
        start_q = jnp.where(pos_q >= end, end, start_q)

    acc[...] = jnp.zeros_like(acc)
    top[...] = jnp.full_like(top, LOW)
    mass[...] = jnp.zeros_like(mass)
    lane = lax.broadcasted_iota(jnp.int32, (16, 128), 1)
    row = lax.broadcasted_iota(jnp.int32, (128, 1), 0)

    def absorb(places, mine=False, cols=slice(0, 1024)):
        amount = 128 * len(places)
        for n, p in enumerate(places):
            b = block(*p)
            for q in range(4):
                if mine and n == 0:
                    feats, tile = own[q, 0:128, :], own[q, 128:144, :]
                else:
                    feats, tile = g_ref[q, b, 0:128, :], g_ref[q, b, 128:144, :]
                keys_ref[128 * n : 128 * n + 128, 128 * q : 128 * q + 128] = feats
                zero = jnp.zeros_like(tile)
                r = 128 * n + 16 * q
                keys_ref[r : r + 16, 512:640] = jnp.where(lane < 64, tile, zero)
                keys_ref[r + 64 : r + 80, 512:640] = jnp.where(lane < 64, zero, tile)
            tag = mate if mine and n == 1 else tags.at[place(*p)]
            pos_k = jnp.where(row < 64, tag[0:1, 0:1] + row, tag[0:1, 64:65] + row - 64)
            hidden = jnp.where((pos_k <= pos_q) & (pos_k >= start_q), 0.0, LOW).astype(BF16)
            keys_ref[128 * n : 128 * n + 128, 640:768] = hidden
        keys = keys_ref[0:amount, :]
        scores = jnp.dot(keys, qt[:, cols], preferred_element_type=F32)
        top_old = top[:, cols]
        top_new = jnp.maximum(top_old, jnp.max(scores, axis=0, keepdims=True))
        weights = jnp.exp2((scores - top_new) * log2e)
        fade = jnp.exp2((top_old - top_new) * log2e)
        mass[:, cols] = mass[:, cols] * fade + jnp.sum(weights, axis=0, keepdims=True)
        acc[:, cols] = acc[:, cols] * fade + lax.dot_general(
            keys[:, 0:512], weights.astype(BF16), (((0,), (0,)), ((), ())), preferred_element_type=F32
        )
        top[:, cols] = top_new

    def absorb_both(*places, cols=slice(0, 1024)):
        absorb([(dz, ox, c) for dz, ox in places for c in range(2)], cols=cols)

    def sib_got(*places):
        for dz, ox in places:
            got(f"s:{dz},{ox}")

    def z_far():
        for dz, dev in ((-3, xp), (3, xm)):
            got(f"z:{dz}")
            y_out(dz, 0)
            fwd(f"x:{dz}", quarter(dz), dev)
        got("z:4")
        y_out(4, 0)
        fwd("x4a", quarter(4).at[0:80], xp)
        fwd("x4b", quarter(4).at[80:144], xm)

    def x_far():
        for dz in (-3, 3):
            got(f"x:{dz}")
            y_out(dz, 1)
        got("x4a")
        got("x4b")
        y_out(4, 1)

    def z_near(n):
        for dz, ahead, side in ((-n, up, xp), (n, down, xm)):
            got(f"z:{dz}")
            if n == 1:
                fwd(f"z:{2 * dz}", whole(dz), ahead)
            fwd(f"x:{dz}", whole(dz), side)
            fwd(f"s:{dz},0", whole(dz), sib)

    def x_near(n):
        if n == 0:
            got("x0a")
            got("x0b")
            fwd("s:0,1", whole(0, 1), sib)
        else:
            for dz in (-n, n):
                got(f"x:{dz}")
                fwd(f"s:{dz},1", whole(dz, 1), sib)

    def y_far(other_x):
        for dz in (-3, 3, 4):
            y_done(dz, other_x)

    def tags_z():
        for n in range(7):
            tag_copies[n].wait_recv()
        send_tag(tags.at[k, xlo], xp)

    def tags_x():
        tag_copies[8].wait_recv()
        send_tag(tags.at[k], sib)

    def take(*places):
        sib_got(*places)
        absorb_both(*places)

    sib_got((0, 0))
    tag_copies[7].wait_recv()
    absorb([(0, 0, 0), (0, 0, 1)], mine=True)
    x_near(0)
    tags_z()
    z_near(1)
    tags_x()
    tag_copies[9].wait_recv()
    take((0, 1))
    z_far()
    x_near(1)
    take((-1, 0), (1, 0))
    z_near(2)
    x_far()
    take((-1, 1), (1, 1))
    y_far(0)
    take((-2, 0), (2, 0))
    x_near(2)
    halves = (slice(0, 512), slice(512, 1024))
    far = [[(dz, ox) for dz in (-3, 3, 4)] for ox in range(2)]
    last = [(-2, 1), (2, 1)]
    sib_got(*far[0])
    absorb_both(*far[0], cols=halves[0])
    y_far(1)
    absorb_both(*far[0], cols=halves[1])
    sib_got(*last)
    absorb_both(*last, cols=halves[0])
    sib_got(*far[1])
    absorb_both(*far[1], cols=halves[0])

    me = device(x, y, z, k)[1]
    sent = {}

    def project(s):
        for pair in range(4):
            cols = slice(512 * s + 128 * pair, 512 * s + 128 * pair + 128)
            context = (acc[:, cols] * (1.0 / mass[:, cols])).astype(BF16)
            for n in range(2):
                h = 2 * pair + n
                value = lax.dot_general(context, w_uv_ref[h], (((0,), (0,)), ((), ())), preferred_element_type=F32)
                att[64 * s : 64 * s + 64, 128 * h : 128 * h + 128] = value[64 * n : 64 * n + 64].astype(BF16)
        for c, (begin, end) in enumerate(COLUMNS):
            width = (end - begin) // 2
            share = jnp.dot(att[64 * s : 64 * s + 64, :], w_out_ref[:, begin:end], preferred_element_type=F32)
            share = share.reshape(8, 8, 2 * width)
            share = jnp.concatenate([share[:, :, :width], share[:, :, width:]], axis=1)
            cols = slice(begin // 2, end // 2)
            part[s, :, cols] = share.reshape(128, width).astype(BF16)
            for n, d in enumerate(peers):
                cp = pltpu.make_async_remote_copy(
                    src_ref=part.at[s, pl.ds(pl.multiple_of(16 * d[1], 16), 16), pl.ds(begin // 2, width)],
                    dst_ref=shares.at[s, n, :, pl.ds(begin // 2, width)],
                    send_sem=share_send.at[s, c, n],
                    recv_sem=share_recv.at[s, c, n],
                    device_id=d,
                    device_id_type=MESH,
                )
                cp.start()
                sent[s, c, n] = cp

    def total(s, c):
        begin, end = COLUMNS[c]
        cols = slice(begin // 2, end // 2)
        result = part[s, pl.ds(pl.multiple_of(16 * me, 16), 16), cols].astype(F32)
        for n in range(len(peers)):
            sent[s, c, n].wait_recv()
            result = result + shares[s, n, :, cols].astype(F32)
        for n in range(len(peers)):
            sent[s, c, n].wait_send()
        return jnp.concatenate([result[0:8], result[8:16]], axis=1)

    loads[5].wait()
    loads[6].wait()
    project(0)
    absorb_both(*last, cols=halves[1])
    absorb_both(*far[1], cols=halves[1])
    project(1)
    for cp in copies.values():
        cp.wait_send()
    for cp in tag_copies:
        cp.wait_send()
    for c, (begin, end) in enumerate(COLUMNS):
        totals[:, begin:end] = total(0, c)
    for c, (begin, end) in enumerate(COLUMNS):
        out_ref[:, begin:end] = jnp.concatenate([totals[:, begin:end], total(1, c)], axis=0).astype(BF16)


def shards(queries, latent, w_uk, w_uv, w_out, span_ids, seq_lengths):
    scale = 1.0 / math.sqrt(queries.shape[1] // w_uk.shape[0])
    hbm = pl.BlockSpec(memory_space=pl.ANY)
    chunks = len(COLUMNS)
    dma = pltpu.SemaphoreType.DMA
    return pl.pallas_call(
        functools.partial(fused_kernel, scale * math.log2(math.e)),
        name="fused",
        out_shape=jax.ShapeDtypeStruct((16, 3584), BF16),
        in_specs=[hbm] * 7,
        out_specs=pl.BlockSpec(memory_space=pltpu.VMEM),
        scratch_shapes=[
            pltpu.VMEM((4, 32, ROWS, 128), BF16),
            pltpu.VMEM((4, ROWS, 128), BF16),
            pltpu.VMEM((2, 2, 8, 8, 128), jnp.int32),
            pltpu.VMEM((8, 128), jnp.int32),
            pltpu.VMEM((128, 1536), BF16),
            pltpu.VMEM((576, 128), BF16),
            pltpu.VMEM((8, 128, 512), BF16),
            pltpu.VMEM((8, 512, 128), BF16),
            pltpu.VMEM((1024, 3584), BF16),
            pltpu.SMEM((2,), jnp.int32),
            pltpu.SMEM((4,), jnp.int32),
            pltpu.VMEM((768, 1024), BF16),
            pltpu.VMEM((768, 768), BF16),
            pltpu.VMEM((512, 1024), F32),
            pltpu.VMEM((1, 1024), F32),
            pltpu.VMEM((1, 1024), F32),
            pltpu.VMEM((128, 1024), BF16),
            pltpu.VMEM((2, 128, 1792), BF16),
            pltpu.VMEM((2, 7, 16, 1792), BF16),
            pltpu.VMEM((8, 3584), F32),
            dma((51,)),
            dma((51,)),
            dma((10,)),
            dma((10,)),
            dma((2, chunks, 7)),
            dma((2, chunks, 7)),
            dma((7,)),
        ],
        compiler_params=pltpu.CompilerParams(collective_id=1, has_side_effects=True, vmem_limit_bytes=48 << 20),
    )(*map(in_hbm, (queries, latent.T, w_uk, w_uv, w_out, span_ids, seq_lengths)))


def solution(mesh):
    return jax.shard_map(
        shards,
        mesh=mesh,
        in_specs=(
            P("ctx", "head"),
            P("ctx", None),
            P("head", None, None),
            P("head", None, None),
            P("head", None),
            P("ctx"),
            P(),
        ),
        out_specs=P(("ctx", "head"), None),
        check_vma=False,
    )
```

```python
import functools
import math

import jax
import jax.numpy as jnp
from jax import lax
from jax.experimental import pallas as pl
from jax.experimental.pallas import tpu as pltpu
from jax.sharding import PartitionSpec as P

MESH = pl.DeviceIdType.MESH
LOW = -1e30
COLUMNS = ((0, 512), (512, 1536), (1536, 2560), (2560, 3584))
F32 = jnp.float32
BF16 = jnp.bfloat16

ROWS = 144


def coords():
    c = lax.axis_index("ctx")
    h = lax.axis_index("head")
    return (h % 2) * 2 + (c // 2) % 2, h // 2, c // 4, c % 2


def device(x, y, z, k):
    x = (x + 4) % 4
    y = (y + 4) % 4
    z = (z + 8) % 8
    k = k % 2
    return (z * 4 + (x % 2) * 2 + k, y * 2 + x // 2)


def in_hbm(array):
    return pltpu.with_memory_space_constraint(array, pltpu.HBM)


def fused_kernel(
    log2e, q_hbm, latent_hbm, w_uk_hbm, w_uv_hbm, w_out_hbm, ids_hbm, len_hbm, out_ref,
    g_ref, own, tags, mate, q_ref, lat_ref, w_uk_ref, w_uv_ref, w_out_ref, ids_ref, len_ref,
    qt, keys_ref, acc, top, mass, att, part, shares, totals,
    send_sem, recv_sem, tag_send, tag_recv, share_send, share_recv, local_sem,
):
    x, y, z, k = coords()
    xlo = x % 2
    zs = {n: device(x, y, z + n, k) for n in (1, -1, 2, -2, 3, -3, 4)}
    up, down = zs[1], zs[-1]
    xp = device(x + 1, y, z, k)
    xm = device(x - 1, y, z, k)
    ys = {n: device(x, y + n, z, k) for n in (1, 2, 3)}
    sib = device(x, y, z, k + 1)
    peers = [ys[2], ys[1], ys[3]] + [device(x + 2, y + n, z, k) for n in (2, 1, 3, 0)]

    barrier = pltpu.get_barrier_semaphore()
    friends = (*zs.values(), xp, xm, sib, *peers)
    for d in friends:
        pl.semaphore_signal(barrier, inc=1, device_id=d, device_id_type=MESH)

    loads = []
    for n, (src, dst) in enumerate(
        (
            (latent_hbm, lat_ref),
            (ids_hbm, ids_ref),
            (len_hbm, len_ref),
            (q_hbm, q_ref),
            (w_uk_hbm, w_uk_ref),
            (w_uv_hbm, w_uv_ref),
            (w_out_hbm, w_out_ref),
        )
    ):
        cp = pltpu.make_async_copy(src, dst, local_sem.at[n])
        cp.start()
        loads.append(cp)

    loads[0].wait()
    lat = lat_ref[...].T
    for q in range(4):
        own[q, 0:128, :] = lat[:, 128 * q : 128 * q + 128]
    rope = lat[:, 512:576].astype(F32)
    packed = jnp.concatenate([rope[0:64], rope[64:128]], axis=1).astype(BF16)
    for q in range(4):
        own[q, 128:144, :] = packed[16 * q : 16 * q + 16, :]
    loads[1].wait()
    col = lax.broadcasted_iota(jnp.int32, (8, 128), 1)
    tags[k, xlo, z] = jnp.where(col < 64, ids_ref[0] * 64 + col, ids_ref[1] * 64 + col - 64)

    pl.semaphore_wait(barrier, len(friends))

    copies = {}

    def send(name, src, dst, dev):
        n = len(copies)
        cp = pltpu.make_async_remote_copy(
            src_ref=src, dst_ref=dst, send_sem=send_sem.at[n], recv_sem=recv_sem.at[n], device_id=dev, device_id_type=MESH
        )
        cp.start()
        copies[name] = cp

    def got(name):
        copies[name].wait_recv()

    tag_copies = []

    def send_tag(ref, dev, to=None):
        n = len(tag_copies)
        cp = pltpu.make_async_remote_copy(
            src_ref=ref, dst_ref=ref if to is None else to, send_sem=tag_send.at[n], recv_sem=tag_recv.at[n], device_id=dev, device_id_type=MESH
        )
        cp.start()
        tag_copies.append(cp)

    def place(dz, other_x=0, other_core=0):
        return (k + other_core) % 2, (xlo + other_x) % 2, (z + dz + 8) % 8

    def block(dz, other_x=0, other_core=0):
        core, xl, zz = place(dz, other_x, other_core)
        return core * 16 + zz * 2 + xl

    def whole(dz, other_x=0):
        return g_ref.at[:, block(dz, other_x)]

    def fwd(name, ref, dev):
        send(name, ref, ref, dev)

    def quarter(dz, other_x=0):
        return g_ref.at[y, block(dz, other_x)]

    def y_out(dz, other_x):
        for n in (2, 1, 3):
            fwd(f"y{n}:{dz},{other_x}", quarter(dz, other_x), ys[n])

    def y_done(dz, other_x):
        for n in (1, 3, 2):
            got(f"y{n}:{dz},{other_x}")
        fwd(f"s:{dz},{other_x}", whole(dz, other_x), sib)

    g0 = block(0)
    for n in (3, -3, 4, 2, -2, 1, -1):
        send_tag(tags.at[k, xlo, z], zs[n])
    send_tag(tags.at[k, xlo, z], sib, mate)
    send("z:-1", own, whole(0), up)
    send("z:1", own, whole(0), down)
    send("x0a", own.at[0:2], g_ref.at[0:2, g0], xp)
    send("x0b", own.at[2:4], g_ref.at[2:4, g0], xm)
    send("s:0,0", own, whole(0), sib)
    for n in (3, -3, 4):
        send(f"z:{-n if n < 4 else 4}", own.at[y], g_ref.at[y, g0], zs[n])

    loads[3].wait()
    loads[4].wait()

    def half_of(rows, s):
        return [rows[16 * o + 8 * s : 16 * o + 8 * s + 8] for o in range(8)]

    spot = lax.broadcasted_iota(jnp.int32, (128, 128), 1) % 64
    feature = lax.broadcasted_iota(jnp.int32, (128, 128), 0)
    for pair in range(4):
        feats, ropes = [], []
        for h in (2 * pair, 2 * pair + 1):
            qn = q_ref[:, 192 * h : 192 * h + 128]
            qr = q_ref[:, 192 * h + 128 : 192 * h + 192].astype(F32)
            feats.append(jnp.dot(qn, w_uk_ref[h], preferred_element_type=F32))
            ropes.append(jnp.concatenate([qr, qr], axis=1))
        for s in range(2):
            cols = slice(512 * s + 128 * pair, 512 * s + 128 * pair + 128)
            qa = jnp.concatenate(half_of(feats[0], s) + half_of(feats[1], s), axis=0)
            qr = jnp.concatenate(half_of(ropes[0], s) + half_of(ropes[1], s), axis=0)
            qt[0:512, cols] = qa.astype(BF16).T
            qt[512:640, cols] = qr.astype(BF16).T
            token = 16 * (spot // 8) + 8 * s + spot % 8
            qt[640:768, cols] = (feature == token).astype(F32).astype(BF16)

    loads[2].wait()
    pos_q = tags[k, xlo, z, 0:1, :]
    start_q = jnp.zeros((1, 128), jnp.int32)
    end = jnp.int32(0)
    for j in range(3):
        end = end + len_ref[j]
        start_q = jnp.where(pos_q >= end, end, start_q)

    acc[...] = jnp.zeros_like(acc)
    top[...] = jnp.full_like(top, LOW)
    mass[...] = jnp.zeros_like(mass)
    lane = lax.broadcasted_iota(jnp.int32, (16, 128), 1)
    row = lax.broadcasted_iota(jnp.int32, (128, 1), 0)

    def absorb(places, mine=False, cols=slice(0, 1024)):
        amount = 128 * len(places)
        for n, p in enumerate(places):
            b = block(*p)
            for q in range(4):
                if mine and n == 0:
                    feats, tile = own[q, 0:128, :], own[q, 128:144, :]
                else:
                    feats, tile = g_ref[q, b, 0:128, :], g_ref[q, b, 128:144, :]
                keys_ref[128 * n : 128 * n + 128, 128 * q : 128 * q + 128] = feats
                zero = jnp.zeros_like(tile)
                r = 128 * n + 16 * q
                keys_ref[r : r + 16, 512:640] = jnp.where(lane < 64, tile, zero)
                keys_ref[r + 64 : r + 80, 512:640] = jnp.where(lane < 64, zero, tile)
            tag = mate if mine and n == 1 else tags.at[place(*p)]
            pos_k = jnp.where(row < 64, tag[0:1, 0:1] + row, tag[0:1, 64:65] + row - 64)
            hidden = jnp.where((pos_k <= pos_q) & (pos_k >= start_q), 0.0, LOW).astype(BF16)
            keys_ref[128 * n : 128 * n + 128, 640:768] = hidden
        keys = keys_ref[0:amount, :]
        scores = jnp.dot(keys, qt[:, cols], preferred_element_type=F32)
        top_old = top[:, cols]
        top_new = jnp.maximum(top_old, jnp.max(scores, axis=0, keepdims=True))
        weights = jnp.exp2((scores - top_new) * log2e)
        fade = jnp.exp2((top_old - top_new) * log2e)
        mass[:, cols] = mass[:, cols] * fade + jnp.sum(weights, axis=0, keepdims=True)
        acc[:, cols] = acc[:, cols] * fade + lax.dot_general(
            keys[:, 0:512], weights.astype(BF16), (((0,), (0,)), ((), ())), preferred_element_type=F32
        )
        top[:, cols] = top_new

    def absorb_both(*places, cols=slice(0, 1024)):
        absorb([(dz, ox, c) for dz, ox in places for c in range(2)], cols=cols)

    def sib_got(*places):
        for dz, ox in places:
            got(f"s:{dz},{ox}")

    def z_far():
        for dz, dev in ((-3, xp), (3, xm)):
            got(f"z:{dz}")
            y_out(dz, 0)
            fwd(f"x:{dz}", quarter(dz), dev)
        got("z:4")
        y_out(4, 0)
        fwd("x4a", quarter(4).at[0:80], xp)
        fwd("x4b", quarter(4).at[80:144], xm)

    def x_far():
        for dz in (-3, 3):
            got(f"x:{dz}")
            y_out(dz, 1)
        got("x4a")
        got("x4b")
        y_out(4, 1)

    def z_near(n):
        for dz, ahead, side in ((-n, up, xp), (n, down, xm)):
            got(f"z:{dz}")
            if n == 1:
                fwd(f"z:{2 * dz}", whole(dz), ahead)
            fwd(f"x:{dz}", whole(dz), side)
            fwd(f"s:{dz},0", whole(dz), sib)

    def x_near(n):
        if n == 0:
            got("x0a")
            got("x0b")
            fwd("s:0,1", whole(0, 1), sib)
        else:
            for dz in (-n, n):
                got(f"x:{dz}")
                fwd(f"s:{dz},1", whole(dz, 1), sib)

    def y_far(other_x):
        for dz in (-3, 3, 4):
            y_done(dz, other_x)

    def tags_z():
        for n in range(7):
            tag_copies[n].wait_recv()
        send_tag(tags.at[k, xlo], xp)

    def tags_x():
        tag_copies[8].wait_recv()
        send_tag(tags.at[k], sib)

    def take(*places):
        sib_got(*places)
        absorb_both(*places)

    sib_got((0, 0))
    tag_copies[7].wait_recv()
    absorb([(0, 0, 0), (0, 0, 1)], mine=True)
    x_near(0)
    tags_z()
    z_near(1)
    tags_x()
    tag_copies[9].wait_recv()
    take((0, 1))
    z_far()
    x_near(1)
    take((-1, 0), (1, 0))
    z_near(2)
    x_far()
    take((-1, 1), (1, 1))
    y_far(0)
    take((-2, 0), (2, 0))
    x_near(2)
    halves = (slice(0, 512), slice(512, 1024))
    far = [[(dz, ox) for dz in (-3, 3, 4)] for ox in range(2)]
    last = [(-2, 1), (2, 1)]
    sib_got(*far[0])
    absorb_both(*far[0], cols=halves[0])
    y_far(1)
    absorb_both(*far[0], cols=halves[1])
    sib_got(*last)
    absorb_both(*last, cols=halves[0])
    sib_got(*far[1])
    absorb_both(*far[1], cols=halves[0])

    me = device(x, y, z, k)[1]

    def project(s):
        for pair in range(4):
            cols = slice(512 * s + 128 * pair, 512 * s + 128 * pair + 128)
            context = (acc[:, cols] * (1.0 / mass[:, cols])).astype(BF16)
            for n in range(2):
                h = 2 * pair + n
                value = lax.dot_general(context, w_uv_ref[h], (((0,), (0,)), ((), ())), preferred_element_type=F32)
                att[64 * s : 64 * s + 64, 128 * h : 128 * h + 128] = value[64 * n : 64 * n + 64].astype(BF16)
        for c, (begin, end) in enumerate(COLUMNS):
            width = (end - begin) // 2
            share = jnp.dot(att[64 * s : 64 * s + 64, :], w_out_ref[:, begin:end], preferred_element_type=F32)
            share = share.reshape(8, 8, 2 * width)
            share = jnp.concatenate([share[:, :, :width], share[:, :, width:]], axis=1)
            cols = slice(begin // 2, end // 2)
            part[s, :, cols] = share.reshape(128, width).astype(BF16)
            for n, d in enumerate(peers):
                cp = pltpu.make_async_remote_copy(
                    src_ref=part.at[s, pl.ds(pl.multiple_of(16 * d[1], 16), 16), pl.ds(begin // 2, width)],
                    dst_ref=shares.at[s, n, :, pl.ds(begin // 2, width)],
                    send_sem=share_send.at[s, c],
                    recv_sem=share_recv.at[s, c],
                    device_id=d,
                    device_id_type=MESH,
                )
                cp.start()

    def total(s, c):
        begin, end = COLUMNS[c]
        cols = slice(begin // 2, end // 2)
        result = part[s, pl.ds(pl.multiple_of(16 * me, 16), 16), cols].astype(F32)
        arrived = shares.at[s, :, :, pl.ds(begin // 2, (end - begin) // 2)]
        pltpu.make_async_copy(arrived, arrived, share_recv.at[s, c]).wait()
        for n in range(len(peers)):
            result = result + shares[s, n, :, cols].astype(F32)
        left = part.at[s, pl.ds(0, 16 * len(peers)), pl.ds(begin // 2, (end - begin) // 2)]
        pltpu.make_async_copy(left, left, share_send.at[s, c]).wait()
        return jnp.concatenate([result[0:8], result[8:16]], axis=1)

    loads[5].wait()
    loads[6].wait()
    project(0)
    absorb_both(*last, cols=halves[1])
    absorb_both(*far[1], cols=halves[1])
    project(1)
    for cp in copies.values():
        cp.wait_send()
    for cp in tag_copies:
        cp.wait_send()
    for c, (begin, end) in enumerate(COLUMNS):
        totals[:, begin:end] = total(0, c)
    for c, (begin, end) in enumerate(COLUMNS):
        out_ref[:, begin:end] = jnp.concatenate([totals[:, begin:end], total(1, c)], axis=0).astype(BF16)


def shards(queries, latent, w_uk, w_uv, w_out, span_ids, seq_lengths):
    scale = 1.0 / math.sqrt(queries.shape[1] // w_uk.shape[0])
    hbm = pl.BlockSpec(memory_space=pl.ANY)
    chunks = len(COLUMNS)
    dma = pltpu.SemaphoreType.DMA
    return pl.pallas_call(
        functools.partial(fused_kernel, scale * math.log2(math.e)),
        name="fused",
        out_shape=jax.ShapeDtypeStruct((16, 3584), BF16),
        in_specs=[hbm] * 7,
        out_specs=pl.BlockSpec(memory_space=pltpu.VMEM),
        scratch_shapes=[
            pltpu.VMEM((4, 32, ROWS, 128), BF16),
            pltpu.VMEM((4, ROWS, 128), BF16),
            pltpu.VMEM((2, 2, 8, 8, 128), jnp.int32),
            pltpu.VMEM((8, 128), jnp.int32),
            pltpu.VMEM((128, 1536), BF16),
            pltpu.VMEM((576, 128), BF16),
            pltpu.VMEM((8, 128, 512), BF16),
            pltpu.VMEM((8, 512, 128), BF16),
            pltpu.VMEM((1024, 3584), BF16),
            pltpu.SMEM((2,), jnp.int32),
            pltpu.SMEM((4,), jnp.int32),
            pltpu.VMEM((768, 1024), BF16),
            pltpu.VMEM((768, 768), BF16),
            pltpu.VMEM((512, 1024), F32),
            pltpu.VMEM((1, 1024), F32),
            pltpu.VMEM((1, 1024), F32),
            pltpu.VMEM((128, 1024), BF16),
            pltpu.VMEM((2, 128, 1792), BF16),
            pltpu.VMEM((2, 7, 16, 1792), BF16),
            pltpu.VMEM((8, 3584), F32),
            dma((51,)),
            dma((51,)),
            dma((10,)),
            dma((10,)),
            dma((2, chunks)),
            dma((2, chunks)),
            dma((7,)),
        ],
        compiler_params=pltpu.CompilerParams(collective_id=1, has_side_effects=True, vmem_limit_bytes=48 << 20),
    )(*map(in_hbm, (queries, latent.T, w_uk, w_uv, w_out, span_ids, seq_lengths)))


def solution(mesh):
    return jax.shard_map(
        shards,
        mesh=mesh,
        in_specs=(
            P("ctx", "head"),
            P("ctx", None),
            P("head", None, None),
            P("head", None, None),
            P("head", None),
            P("ctx"),
            P(),
        ),
        out_specs=P(("ctx", "head"), None),
        check_vma=False,
    )
```
